32 devices in a mesh: wave: 4 (over z), lev: 8 (over y, x, core).
Axes of the slice: x: 2, y: 2, z: 4, core: 2. Of those that a mesh axis runs over, the one named last changes fastest.
Arguments:
- grid_values: bfloat16 [256, 480, 1024], P('lev', 'wave'), may hold values from -6 to 6
- legendre: bfloat16 [160, 480, 384], P('wave'), as said below
- gauss_weights: float32 [480], replicated, may hold values from 0.5 to 1.5
- modes_in: bfloat16 [128, 128], replicated, may hold values from -0.5 to 0.5
- modes_out: bfloat16 [128, 128], replicated, may hold values from -0.5 to 0.5
- stiffness: float32 [128], replicated, may hold values from 0.1 to 10
- slot_pair: int32 [160], replicated, may hold values from 0 to 159, each once
- lat_order: int32 [480], replicated, may hold values from 0 to 479, each once
- field_slots: int32 [256], replicated, may hold values from 0 to 255, each once
Outputs:
- product: bfloat16 [256, 480, 1024], P('lev', 'wave')
The draws below stay inside these ranges and needn't reach their ends.
Inputs may be any that keep to these rules, and one draw needn't show every extreme that they name: legendre is zero in every column c > 320. `slot_pair`: a permutation. `lat_order`: a permutation. `field_slots`: a permutation.
All inputs are finite; a program needn't handle non-finite values.
Results may differ from the reference program's by a relative error of at most 0.0085.
Values may be sent and summed in bfloat16 or wider, within the bound.
No kernel may reach another device: no remote copies, remote signals or barrier semaphores. Data moves between devices by JAX's collectives and lax.ppermute only.
A program may use at most 128 MiB of HBM per device.

```python
import math
import jax
import jax.numpy as jnp
from jax import lax

NLAT = 480
NLON = 1024
NM = 320
LEVELS = 128
PAIRS = 160
KP = 384
FL = 256


def draw_legendre(key, part):
    array_shape = (PAIRS, NLAT, KP)
    values = jnp.clip(jax.random.normal(key, array_shape, jnp.float32), -6.0, 6.0) / math.sqrt(NLAT)
    valid_column = jnp.arange(KP) <= NM
    return jnp.where(valid_column[None, None, :], values, 0.0).astype(jnp.bfloat16)


def shard_levels(own_key, shape, pieces, low, top_value):
    def one(axis_at, parts):
        heights = jax.random.uniform(jax.random.fold_in(jax.random.fold_in(own_key, 6), axis_at), (parts,), jnp.float32, low / len(pieces), top_value / len(pieces))
        return jnp.repeat(jnp.exp(heights), shape[axis_at] // parts).reshape((-1,) + (1,) * (len(shape) - axis_at - 1))

    factor_of = one(*pieces[0])
    for cut in pieces[1:]:
        factor_of = factor_of * one(*cut)
    return factor_of


def centred(own_key, shape, spread, reach, cuts=(), held_as=jnp.bfloat16):
    gain = shard_levels(own_key, shape, cuts, -0.22, 0.18) if cuts else 1.0
    drawn = jax.random.normal(own_key, shape, jnp.float32) * spread * gain
    return jnp.minimum(jnp.maximum(drawn, -reach), reach).astype(held_as)


def setup_inputs(seed: int = 0) -> dict:
    seeds = jax.random.split(jax.random.key(seed), 10)
    return {
        "grid_values": centred(seeds[0], (FL, NLAT, NLON), 1.0, 6.0, ((0, 8), (1, 4))),
        "legendre": draw_legendre(jax.random.fold_in(seeds[9], 71), 0),
        "gauss_weights": jnp.clip(jax.random.uniform(seeds[2], (NLAT,), jnp.float32, 0.5, 1.5), 0.5, 1.5),
        "modes_in": centred(seeds[3], (LEVELS, LEVELS), LEVELS ** -0.5, 0.5),
        "modes_out": centred(seeds[4], (LEVELS, LEVELS), LEVELS ** -0.5, 0.5),
        "stiffness": jnp.clip(jnp.exp(jax.random.uniform(seeds[5], (LEVELS,), jnp.float32, math.log(0.1), math.log(10.0))), 0.1, 10.0),
        "slot_pair": jax.random.permutation(seeds[6], PAIRS).astype(jnp.int32),
        "lat_order": jax.random.permutation(seeds[7], NLAT).astype(jnp.int32),
        "field_slots": jax.random.permutation(seeds[8], FL).astype(jnp.int32),
    }


def fourier_table(wavenumbers, longitudes):
    lon_index = jnp.arange(longitudes, dtype=jnp.int32)
    phase_steps = lon_index[:, None] * wavenumbers[None, :] % longitudes
    angles = phase_steps.astype(jnp.float32) * (2.0 * jnp.pi / longitudes)
    scaling = 1.0 / jnp.sqrt(jnp.float32(longitudes))
    entries = jnp.stack([jnp.cos(angles), -jnp.sin(angles)], axis=2) * scaling
    return entries.astype(jnp.bfloat16).reshape(longitudes, 2 * wavenumbers.shape[0])

def reference(grid_values, legendre, gauss_weights, modes_in, modes_out, stiffness, slot_pair, lat_order, field_slots):
    row_count, lat_count, lon_count = grid_values.shape
    column_count = legendre.shape[2]
    wave_table = fourier_table(jnp.arange(NM, dtype=jnp.int32), lon_count)
    row_weight = gauss_weights[lat_order]
    fourier = jnp.dot(grid_values.reshape(row_count * lat_count, lon_count), wave_table, preferred_element_type=jnp.float32)
    fourier = (fourier.reshape(row_count, lat_count, NM, 2) * row_weight[None, :, None, None]).astype(jnp.bfloat16)
    fourier_true = jnp.zeros_like(fourier).at[:, lat_order].set(fourier)
    column = jnp.arange(column_count, dtype=jnp.int32)

    def forward_slot(inputs):
        basis_slot, pair_index = inputs
        first_half = column < NM - pair_index
        basis_wide = basis_slot.astype(jnp.float32)
        lower_wave = jnp.take(fourier_true, pair_index, axis=2).astype(jnp.float32)
        upper_wave = jnp.take(fourier_true, NM - 1 - pair_index, axis=2).astype(jnp.float32)
        lower_part = jnp.einsum('rji,jc->ric', lower_wave, basis_wide)
        upper_part = jnp.einsum('rji,jc->ric', upper_wave, basis_wide)
        return jnp.where(first_half, lower_part, upper_part).astype(jnp.bfloat16)
    spectral = lax.map(forward_slot, (legendre, slot_pair))
    spectral_rows = jnp.moveaxis(spectral, 0, 1)
    ordered = jnp.zeros_like(spectral_rows).at[field_slots].set(spectral_rows)
    pair_column = slot_pair[:, None]
    degree = jnp.where(column[None, :] < NM - pair_column, pair_column + column[None, :], column[None, :] - 1).astype(jnp.float32)
    growth = degree * (degree + 1.0) / (NM * NM)
    factor = 1.0 / (1.0 + growth[None, :, None, :] * stiffness[:, None, None, None])
    fields_count = row_count // LEVELS
    stacked = ordered.reshape(fields_count, LEVELS, slot_pair.shape[0], 2, column_count).astype(jnp.float32)
    projected = jnp.einsum('ml,flkic->fmkic', modes_in.astype(jnp.float32), stacked)
    modal_values = (projected * factor[None]).astype(jnp.bfloat16)
    restored = jnp.einsum('lm,fmkic->flkic', modes_out.astype(jnp.float32), modal_values.astype(jnp.float32)).astype(jnp.bfloat16)
    implicit = restored.reshape(row_count, slot_pair.shape[0], 2, column_count)[field_slots]

    def backward_slot(inputs):
        basis_slot, pair_index, coefficients = inputs
        first_half = column < NM - pair_index
        basis_wide = basis_slot.astype(jnp.float32)
        coeff_wide = coefficients.astype(jnp.float32)
        lower_part = jnp.einsum('ric,jc->rji', jnp.where(first_half, coeff_wide, 0.0), basis_wide)
        upper_part = jnp.einsum('ric,jc->rji', jnp.where(first_half, 0.0, coeff_wide), basis_wide)
        return (lower_part.astype(jnp.bfloat16), upper_part.astype(jnp.bfloat16))
    lower_all, upper_all = lax.map(backward_slot, (legendre, slot_pair, jnp.moveaxis(implicit, 1, 0)))
    back_true = jnp.zeros((row_count, lat_count, NM, 2), jnp.bfloat16)
    back_true = back_true.at[:, :, slot_pair].set(jnp.moveaxis(lower_all, 0, 2))
    back_true = back_true.at[:, :, NM - 1 - slot_pair].set(jnp.moveaxis(upper_all, 0, 2))
    fourier_back = back_true[:, lat_order]
    field_values = lax.dot_general(fourier_back.reshape(row_count * lat_count, 2 * NM), wave_table, (((1,), (1,)), ((), ())), preferred_element_type=jnp.float32)
    product = field_values.reshape(row_count, lat_count, lon_count) * grid_values.astype(jnp.float32)
    return product.astype(jnp.bfloat16)
```

```python
import functools
import math

import jax
import jax.numpy as jnp
from jax import lax
from jax.experimental import pallas as pl
from jax.experimental.pallas import tpu as pltpu
from jax.sharding import PartitionSpec as P

VMEM_LIMIT = 56 * 1024 * 1024


def round_up(value, unit):
    return -(-value // unit) * unit


def params(steps):
    return pltpu.CompilerParams(
        dimension_semantics=("arbitrary",) * steps, vmem_limit_bytes=VMEM_LIMIT
    )


def cost(flops, moved):
    return pl.CostEstimate(flops=int(flops), bytes_accessed=int(moved), transcendentals=0)


def dot(left, right, dims):
    return lax.dot_general(left, right, (dims, ((), ())), preferred_element_type=jnp.float32)


def modulo(values, size):
    return values & (size - 1) if size & (size - 1) == 0 else lax.rem(values, size)


def half_table(wavenumbers, longitudes):
    lon = jnp.arange(longitudes // 2, dtype=jnp.int32)
    turn = jnp.arange(2, dtype=jnp.int32) * (longitudes // 4)
    steps = wavenumbers[:, None, :, None] * lon + turn[:, None, None]
    steps = modulo(steps, longitudes)
    eighth = longitudes // 8
    quarter = (
        (steps >= eighth).astype(jnp.int32)
        + (steps >= 3 * eighth).astype(jnp.int32)
        + (steps >= 5 * eighth).astype(jnp.int32)
        + (steps >= 7 * eighth).astype(jnp.int32)
    )
    angle = (steps - quarter * (2 * eighth)).astype(jnp.float32) * (2.0 * math.pi / longitudes)
    square = angle * angle
    cosine = 1.0 + square * (
        -0.5 + square * (1.0 / 24 + square * (-1.0 / 720 + square * (1.0 / 40320)))
    )
    sine = angle * (
        1.0 + square * (-1.0 / 6 + square * (1.0 / 120 + square * (-1.0 / 5040 + square / 362880)))
    )
    value = jnp.where((quarter & 1) == 0, cosine, sine)
    value = jnp.where((quarter == 1) | (quarter == 2), -value, value)
    scaled = value * (1.0 / math.sqrt(longitudes))
    return scaled.astype(jnp.bfloat16).reshape(2, -1, longitudes // 2)


def row_block(row_count):
    return 16 if row_count % 16 == 0 else row_count


def fourier_kernel(grid_ref, table_ref, weight_ref, *rest):
    held = rest[-1]
    rows, lats, lons = grid_ref.shape
    slots = table_ref.shape[1] // 2
    wide = held.shape[-1]
    half = lons // 2
    stride = 4 * rows + 1

    def one(pair, carry):
        both = []
        for side in range(2):
            block = grid_ref[pair * 2 + side]
            if wide > lats:
                block = jnp.concatenate([block, jnp.zeros((wide - lats, lons), block.dtype)], axis=0)
            both.append(block)
        stacked = jnp.concatenate(both, axis=0)
        low, high = stacked[:, :half], stacked[:, half:]
        for parity in range(2):
            folded = low + high if parity == 0 else low - high
            made = dot(table_ref[parity], folded, ((1,), (1,)))
            for side in range(2):
                for q in range(2):
                    piece = made[q * slots : (q + 1) * slots, side * wide : (side + 1) * wide]
                    start = parity * 2 * rows + q * rows + pair * 2 + side
                    held[pl.ds(start, slots, stride=stride), :] = piece * weight_ref[...]
        return carry

    lax.fori_loop(0, rows // 2, one, 0, unroll=2 if rows % 4 == 0 else 1)
    base = 0
    for out_ref in rest[:-1]:

        def put(slot, carry, base=base, out_ref=out_ref):
            value = held[pl.ds((base + slot) * stride, 4 * rows), :]
            out_ref[slot] = value.reshape(2, 2, rows, wide).astype(jnp.bfloat16)
            return carry

        lax.fori_loop(0, out_ref.shape[0], put, 0, unroll=2)
        base += out_ref.shape[0]


def fourier(grid_values, table, weight, counts, wide):
    rows, lats, lons = grid_values.shape
    slots = sum(counts)
    block = row_block(rows)
    return pl.pallas_call(
        fourier_kernel,
        grid=(rows // block,),
        in_specs=[
            pl.BlockSpec((block, lats, lons), lambda b: (b, 0, 0)),
            pl.BlockSpec(table.shape, lambda b: (0, 0, 0)),
            pl.BlockSpec(weight.shape, lambda b: (0, 0)),
        ],
        out_specs=[pl.BlockSpec((n, 2, 2, block, wide), lambda b: (0, 0, 0, b, 0)) for n in counts],
        out_shape=[jax.ShapeDtypeStruct((n, 2, 2, rows, wide), jnp.bfloat16) for n in counts],
        scratch_shapes=[pltpu.VMEM((slots * (4 * block + 1), wide), jnp.float32)],
        compiler_params=params(1),
        cost_estimate=cost(
            rows * lats * lons * slots * 4, rows * lats * lons * 2 + slots * rows * wide * 8
        ),
    )(grid_values, table, weight)


def basis_kernel(first_ref, basis_ref, lats_ref, out_ref):
    keep = out_ref.shape[1]
    size = (basis_ref.shape[1], out_ref.shape[2])
    hit = lax.broadcasted_iota(jnp.int32, size, 0) == lats_ref[0]
    order = jnp.where(hit, 1.0, 0.0).astype(jnp.bfloat16)
    for j in range(basis_ref.shape[0]):
        made = dot(basis_ref[j], order, ((0,), (0,)))
        out_ref[j] = made[:keep].astype(jnp.bfloat16)


def ordered_basis(basis, lats, keep, block, first, count):
    _, lat_count, columns = basis.shape
    wide = lats.shape[1]
    return pl.pallas_call(
        basis_kernel,
        grid_spec=pltpu.PrefetchScalarGridSpec(
            num_scalar_prefetch=1,
            grid=(count,),
            in_specs=[
                pl.BlockSpec((block, lat_count, columns), lambda i, first: (first[0] + i, 0, 0)),
                pl.BlockSpec((1, 1, wide), lambda i, first: (0, 0, 0)),
            ],
            out_specs=pl.BlockSpec((block, keep, wide), lambda i, first: (i, 0, 0)),
        ),
        out_shape=jax.ShapeDtypeStruct((count * block, keep, wide), jnp.bfloat16),
        compiler_params=params(1),
        cost_estimate=cost(
            2 * count * block * lat_count * columns * wide,
            count * block * (lat_count * columns + keep * wide) * 2,
        ),
    )(first, basis, lats[:, None, :])


def first_side(pair, waves, shape):
    column = lax.broadcasted_iota(jnp.int32, shape, 0)
    odd = pair & 1
    sign = 1 - 2 * odd
    return column * sign < (waves - pair) * sign + odd


def sums_of_pair(waves, pairs, values, bases):
    halves = []
    for j in range(2):
        made = dot(bases[j], values[j], ((1,), (1,)))
        width = made.shape[1] // 2
        side = first_side(pairs[j], waves, (made.shape[0], width))
        halves.append(jnp.where(side, made[:, :width], made[:, width:]))
    return jnp.concatenate(halves, axis=1)


def fields_of_pair(waves, pairs, coeff, bases):
    width = coeff.shape[1] // 2
    made = []
    for j in range(2):
        part = coeff[:, j * width : (j + 1) * width]
        side = first_side(pairs[j], waves, part.shape)
        empty = jnp.zeros_like(part)
        spread = jnp.concatenate(
            [jnp.where(side, part, empty), jnp.where(side, empty, part)], axis=1
        ).astype(jnp.bfloat16)
        made.append(dot(spread, bases[j], ((0,), (0,))).astype(jnp.bfloat16))
    return made


def sums_kernel(waves, base, blocks, pairs_ref, *rest):
    coeff_refs, basis_ref, out_ref = rest[:blocks], rest[blocks], rest[blocks + 1]
    parts = basis_ref.shape[1]
    start = base + pl.program_id(0) * parts
    for e in range(parts // 2):
        total = sums_of_pair(
            waves,
            [pairs_ref[start + 2 * e + j] for j in range(2)],
            [jnp.concatenate([ref[0, 2 * e + j] for ref in coeff_refs], axis=1) for j in range(2)],
            [basis_ref[0, 2 * e + j] for j in range(2)],
        )
        out_ref[0, e] = total.astype(jnp.bfloat16)


def fields_kernel(waves, base, pairs_ref, coeff_ref, basis_ref, *out_refs):
    parts, wide = basis_ref.shape[1], out_refs[0].shape[3]
    start = base + pl.program_id(0) * parts
    for e in range(parts // 2):
        made = fields_of_pair(
            waves,
            [pairs_ref[start + 2 * e + j] for j in range(2)],
            coeff_ref[0, e].astype(jnp.float32),
            [basis_ref[0, 2 * e + j] for j in range(2)],
        )
        for j in range(2):
            for u, ref in enumerate(out_refs):
                ref[0, 2 * e + j] = made[j][:, u * wide : (u + 1) * wide]


def legendre_call(kernel, scalars, operands, specs, shapes, out_specs, steps, slots, keep, depth, wide):
    return pl.pallas_call(
        kernel,
        grid_spec=pltpu.PrefetchScalarGridSpec(
            num_scalar_prefetch=len(scalars),
            grid=(steps,),
            in_specs=specs,
            out_specs=out_specs,
        ),
        out_shape=[jax.ShapeDtypeStruct(shape, jnp.bfloat16) for shape in shapes],
        compiler_params=params(1),
        cost_estimate=cost(
            4 * slots * keep * depth * wide, 4 * slots * (keep * wide + depth * wide)
        ),
    )(*scalars, *operands)


def step_spec(shape, at):
    block = tuple(1 if d == at else size for d, size in enumerate(shape))
    return pl.BlockSpec(block, lambda i, *s: tuple(i if d == at else 0 for d in range(len(shape))))


def own_spec(basis, low):
    _, parts, keep, wide = basis.shape
    return pl.BlockSpec((1, parts, keep, wide), lambda i, *s: (low + i, 0, 0, 0))


def sums(waves, base, pairs, coeffs, basis, low):
    steps, parts, depth, wide = coeffs[0].shape
    keep = basis.shape[2]
    shape = (steps, parts // 2, keep, depth)
    return legendre_call(
        functools.partial(sums_kernel, waves, base, len(coeffs)),
        [pairs],
        [*coeffs, basis],
        [step_spec(x.shape, 0) for x in coeffs] + [own_spec(basis, low)],
        [shape],
        [step_spec(shape, 0)],
        steps, steps * parts, keep, depth, wide * len(coeffs),
    )[0]


def fields(waves, base, pairs, coeff, basis, low, blocks):
    steps, half_parts, keep, depth = coeff.shape
    wide = basis.shape[3] // blocks
    shape = (steps, 2 * half_parts, depth, wide)
    return legendre_call(
        functools.partial(fields_kernel, waves, base),
        [pairs],
        [coeff, basis],
        [step_spec(coeff.shape, 0), own_spec(basis, low)],
        [shape] * blocks,
        [step_spec(shape, 0)] * blocks,
        steps, steps * 2 * half_parts, keep, depth, wide * blocks,
    )


def matrices_kernel(lev_size, slot_ref, modes_in_ref, modes_out_ref, stiff_ref, in_ref, out_ref, row_ref):
    levels = modes_in_ref.shape[0]
    fields = in_ref.shape[2] // (4 * levels)
    rows = slot_ref.shape[0] // lev_size
    depth = 4 * rows
    lane = lax.broadcasted_iota(jnp.int32, (slot_ref.shape[0], levels), 1)
    hits = [slot_ref[...] - f * levels == lane for f in range(fields)]
    own = [jnp.where(hit, 1.0, 0.0).astype(jnp.bfloat16) for hit in hits]
    row_ref[...] = jnp.concatenate([stiff_ref[...]] * (4 * fields), axis=1)
    for target, modes, side in ((in_ref, modes_in_ref, 1), (out_ref, modes_out_ref, 0)):
        made = jnp.concatenate([dot(hit, modes[...], ((1,), (side,))) for hit in own], axis=1)
        empty = jnp.zeros((rows, made.shape[1]), jnp.float32)
        for v in range(lev_size):
            block = made[v * rows : (v + 1) * rows]
            lines = [
                jnp.concatenate([block if g == h else empty for h in range(4)], axis=1)
                for g in range(4)
            ]
            target[v] = jnp.concatenate(lines, axis=0).astype(jnp.bfloat16)


def matrices(field_slots, modes_in, modes_out, stiffness, lev_size):
    total, levels = field_slots.shape[0], modes_in.shape[0]
    shape = (lev_size, 4 * total // lev_size, 4 * total)
    return pl.pallas_call(
        functools.partial(matrices_kernel, lev_size),
        out_shape=[
            jax.ShapeDtypeStruct(shape, jnp.bfloat16),
            jax.ShapeDtypeStruct(shape, jnp.bfloat16),
            jax.ShapeDtypeStruct((1, 4 * total), jnp.float32),
        ],
        compiler_params=pltpu.CompilerParams(vmem_limit_bytes=VMEM_LIMIT),
        cost_estimate=cost(0, 4 * math.prod(shape)),
    )(field_slots[:, None], modes_in, modes_out, stiffness[None, :])


def solve_kernel(waves, base, keep, count, rank_ref, pairs_ref, arrived_ref, in_ref, out_of_ref, stiff_ref, out_ref):
    sources, share, _ = arrived_ref.shape
    total = dot(arrived_ref[0], in_ref[0], ((1,), (0,)))
    for source in range(1, sources):
        total = total + dot(arrived_ref[source], in_ref[source], ((1,), (0,)))
    width = total.shape[1] // 2
    place = rank_ref[0] * share + lax.broadcasted_iota(jnp.int32, (share, 1), 0)
    factors = []
    for j in range(2):
        column = place
        pair = jnp.zeros_like(place) + pairs_ref[base + j]
        for e in range(1, count):
            column = jnp.where(place >= e * keep, place - e * keep, column)
            pair = jnp.where(place >= e * keep, pairs_ref[base + 2 * e + j], pair)
        degree = jnp.where(column < waves - pair, pair + column, column - 1).astype(jnp.float32)
        growth = degree * (degree + 1.0) * (1.0 / (waves * waves))
        factors.append(1.0 / (1.0 + growth * stiff_ref[:, j * width : (j + 1) * width]))
    modal = (total * jnp.concatenate(factors, axis=1)).astype(jnp.bfloat16)
    for source in range(sources):
        out_ref[source] = dot(modal, out_of_ref[source], ((1,), (1,))).astype(jnp.bfloat16)


def solve(waves, base, keep, count, rank, pairs, arrived, into, out_of, stiff):
    def whole(shape):
        return pl.BlockSpec(shape, lambda i, *s: (0,) * len(shape))

    return pl.pallas_call(
        functools.partial(solve_kernel, waves, base, keep, count),
        grid_spec=pltpu.PrefetchScalarGridSpec(
            num_scalar_prefetch=2,
            grid=(1,),
            in_specs=[whole(x.shape) for x in (arrived, into, out_of, stiff)],
            out_specs=whole(arrived.shape),
        ),
        out_shape=jax.ShapeDtypeStruct(arrived.shape, jnp.bfloat16),
        compiler_params=params(1),
        cost_estimate=cost(
            4 * arrived.size * into.shape[2], 2 * (arrived.size * 2 + into.size * 2)
        ),
    )(rank, pairs, arrived, into, out_of, stiff)


def product_kernel(*refs):
    operands = refs[: len(refs) - 4]
    table_ref, grid_ref, out_ref, held = refs[len(refs) - 4 :]
    rows, lats, lons = grid_ref.shape
    wide = held.shape[-1]
    half = lons // 2
    stride = 4 * rows + 1
    slots = table_ref.shape[1] // 2
    base = 0
    for ref in operands:

        def take(d, carry, ref=ref, base=base):
            value = ref[d].astype(jnp.float32)
            held[pl.ds((base + d) * stride, 4 * rows), :] = value.reshape(4 * rows, wide)
            return carry

        lax.fori_loop(0, ref.shape[0], take, 0, unroll=2)
        base += ref.shape[0]

    def one(pair, carry):
        fields = []
        for parity in range(2):
            sides = []
            for side in range(2):
                start = parity * 2 * rows + pair * 2 + side
                sides.append(
                    jnp.concatenate(
                        [held[pl.ds(start + q * rows, slots, stride=stride), :] for q in range(2)],
                        axis=0,
                    ).astype(jnp.bfloat16)
                )
            fields.append(dot(jnp.concatenate(sides, axis=1), table_ref[parity], ((0,), (0,))))
        low, high = fields[0] + fields[1], fields[0] - fields[1]
        for side in range(2):
            row = pair * 2 + side
            block = grid_ref[row].astype(jnp.float32)
            out_ref[row, :, :half] = (
                low[side * wide : side * wide + lats] * block[:, :half]
            ).astype(jnp.bfloat16)
            out_ref[row, :, half:] = (
                high[side * wide : side * wide + lats] * block[:, half:]
            ).astype(jnp.bfloat16)
        return carry

    lax.fori_loop(0, rows // 2, one, 0)


def grid_product(operands, table, grid_values, wide):
    rows, lats, lons = grid_values.shape
    block = row_block(rows)
    slots = table.shape[1] // 2
    operands = [x.reshape(-1, 2, 2, rows, wide) for x in operands]
    grid_spec = pl.BlockSpec((block, lats, lons), lambda b: (b, 0, 0))
    return pl.pallas_call(
        product_kernel,
        grid=(rows // block,),
        in_specs=[
            pl.BlockSpec(x.shape[:3] + (block, wide), lambda b: (0, 0, 0, b, 0)) for x in operands
        ]
        + [pl.BlockSpec(table.shape, lambda b: (0, 0, 0)), grid_spec],
        out_specs=grid_spec,
        out_shape=jax.ShapeDtypeStruct(grid_values.shape, jnp.bfloat16),
        scratch_shapes=[pltpu.VMEM((slots * (4 * block + 1), wide), jnp.float32)],
        compiler_params=params(1),
        cost_estimate=cost(
            rows * lats * lons * slots * 4, rows * lats * lons * 4 + slots * rows * wide * 8
        ),
    )(*operands, table, grid_values)


PIECES = (1, 2, 2)
BARRIERS = False


def pieces_of(count):
    cuts, at = [], 0
    for size in PIECES:
        if at < count:
            cuts.append((at, min(count, at + size)))
            at += size
    if at < count:
        cuts.append((at, count))
    return cuts


def pick(table, rows):
    hit = rows[:, None] == jnp.arange(table.shape[0], dtype=jnp.int32)[None, :]
    hit = hit.reshape(hit.shape + (1,) * (table.ndim - 1))
    return jnp.sum(jnp.where(hit, table[None], 0), axis=1)


def after(value, *earlier):
    return lax.optimization_barrier((value, *earlier))[0] if BARRIERS else value


def local(
    grid_values,
    legendre,
    gauss_weights,
    modes_in,
    modes_out,
    stiffness,
    slot_pair,
    lat_order,
    field_slots,
):
    rows, lats, lons = grid_values.shape
    slots = legendre.shape[0]
    wave_size, lev_size = lax.axis_size("wave"), lax.axis_size("lev")
    wave_rank, lev_rank = lax.axis_index("wave"), lax.axis_index("lev")
    waves = 2 * slot_pair.shape[0]
    parts = math.gcd(slots, 8)
    chunks = slots // parts
    keep = round_up(waves + 1, 16)
    wide = round_up(lats, 128) if lats > 64 else round_up(lats, 32)
    depth = 4 * rows
    pieces = pieces_of(chunks)

    slot_at, owner_at = [], []
    for low, high in pieces:
        for u in range(wave_size):
            slot_at += range(low * parts, high * parts)
            owner_at += [u] * ((high - low) * parts)
    owner = wave_rank ^ jnp.array(owner_at, dtype=jnp.int32)
    pairs = pick(slot_pair, owner * slots + jnp.array(slot_at, dtype=jnp.int32))
    mirrored = waves - 1 - pairs
    odd_pair = (pairs & 1) == 1
    table = half_table(
        jnp.stack([jnp.where(odd_pair, mirrored, pairs), jnp.where(odd_pair, pairs, mirrored)]), lons
    )

    lat_blocks = jnp.pad(
        lat_order.reshape(wave_size, lats), ((0, 0), (0, wide - lats)), constant_values=-1
    )
    relative = wave_rank ^ jnp.arange(wave_size, dtype=jnp.int32)
    chosen = pick(lat_blocks, relative).reshape(1, -1)
    own_lats = pick(lat_blocks, wave_rank.reshape(1)).reshape(-1)
    row_weight = jnp.sum(
        jnp.where(
            own_lats[None, :] == jnp.arange(lat_order.shape[0], dtype=jnp.int32)[:, None],
            gauss_weights[:, None],
            0.0,
        ),
        axis=0,
        keepdims=True,
    )
    counts = [(high - low) * parts for low, high in pieces for _ in range(wave_size)]
    made = fourier(grid_values, table, row_weight, counts, wide)
    routes = [[(i, i ^ u) for i in range(wave_size)] for u in range(wave_size)]

    def exchange(blocks):
        return [blocks[0]] + [lax.ppermute(blocks[u], "wave", routes[u]) for u in range(1, wave_size)]

    coefficients = []
    for piece, (low, high) in enumerate(pieces):
        blocks = made[piece * wave_size : (piece + 1) * wave_size]
        shape = (high - low, parts, depth, wide)
        coefficients.append(exchange([block.reshape(shape) for block in blocks]))

    basis = ordered_basis(legendre, chosen, keep, chunks, jnp.zeros((1,), jnp.int32), parts)
    basis = basis.reshape(chunks, parts, keep, -1)
    into, out_of, stiff = matrices(field_slots, modes_in, modes_out, stiffness, lev_size)
    rank = lev_rank.reshape(1)

    operands = []
    for piece, (low, high) in enumerate(pieces):
        steps = high - low
        base = low * wave_size * parts
        spectral = sums(waves, base, pairs, coefficients[piece], basis, low)
        flat = steps * (parts // 2) * keep
        padded = round_up(flat, lev_size * 8)
        spectral = spectral.reshape(flat, depth)
        if padded > flat:
            spectral = jnp.pad(spectral, ((0, padded - flat), (0, 0)))
        arrived = lax.all_to_all(
            spectral.reshape(lev_size, -1, depth), "lev", split_axis=0, concat_axis=0, tiled=True
        )
        solved = solve(
            waves, base, keep, steps * (parts // 2), rank, pairs, arrived, into, out_of, stiff
        )
        returned = lax.all_to_all(solved, "lev", split_axis=0, concat_axis=0, tiled=True)
        implicit = returned.reshape(padded, depth)[:flat].reshape(steps, parts // 2, keep, depth)
        operands += exchange(fields(waves, base, pairs, implicit, basis, low, wave_size))
    return grid_product(operands, table, grid_values, wide)


def solution(mesh):
    in_specs = (P("lev", "wave", None), P("wave", None, None), P(), P(), P(), P(), P(), P(), P())
    out_specs = P("lev", "wave", None)
    return jax.shard_map(local, mesh=mesh, in_specs=in_specs, out_specs=out_specs, check_vma=False)
```

```python
import functools
import math

import jax
import jax.numpy as jnp
from jax import lax
from jax.experimental import pallas as pl
from jax.experimental.pallas import tpu as pltpu
from jax.sharding import PartitionSpec as P

SCALE = 10.0
VMEM_LIMIT = 56 * 1024 * 1024


def round_up(value, unit):
    return -(-value // unit) * unit


def params(steps):
    return pltpu.CompilerParams(
        dimension_semantics=("arbitrary",) * steps, vmem_limit_bytes=VMEM_LIMIT
    )


def cost(flops, moved):
    return pl.CostEstimate(flops=int(flops * SCALE), bytes_accessed=int(moved * SCALE), transcendentals=0)


def waiting(kernel, inputs, count):
    def run(*refs):
        kernel(*refs[:inputs], *refs[inputs + count :])

    return run


def wait_specs(earlier):
    return [pl.BlockSpec(memory_space=pl.ANY)] * len(earlier)


def dot(left, right, dims):
    return lax.dot_general(left, right, (dims, ((), ())), preferred_element_type=jnp.float32)


def modulo(values, size):
    return values & (size - 1) if size & (size - 1) == 0 else lax.rem(values, size)


def half_table(wavenumbers, longitudes):
    lon = jnp.arange(longitudes // 2, dtype=jnp.int32)
    turn = jnp.arange(2, dtype=jnp.int32) * (longitudes // 4)
    steps = wavenumbers[:, None, :, None] * lon + turn[:, None, None]
    steps = modulo(steps, longitudes)
    eighth = longitudes // 8
    quarter = (
        (steps >= eighth).astype(jnp.int32)
        + (steps >= 3 * eighth).astype(jnp.int32)
        + (steps >= 5 * eighth).astype(jnp.int32)
        + (steps >= 7 * eighth).astype(jnp.int32)
    )
    angle = (steps - quarter * (2 * eighth)).astype(jnp.float32) * (2.0 * math.pi / longitudes)
    square = angle * angle
    cosine = 1.0 + square * (
        -0.5 + square * (1.0 / 24 + square * (-1.0 / 720 + square * (1.0 / 40320)))
    )
    sine = angle * (
        1.0 + square * (-1.0 / 6 + square * (1.0 / 120 + square * (-1.0 / 5040 + square / 362880)))
    )
    value = jnp.where((quarter & 1) == 0, cosine, sine)
    value = jnp.where((quarter == 1) | (quarter == 2), -value, value)
    scaled = value * (1.0 / math.sqrt(longitudes))
    return scaled.astype(jnp.bfloat16).reshape(2, -1, longitudes // 2)


def row_block(row_count):
    return 16 if row_count % 16 == 0 else row_count


def fourier_kernel(grid_ref, table_ref, weight_ref, *rest):
    held = rest[-1]
    rows, lats, lons = grid_ref.shape
    slots = table_ref.shape[1] // 2
    wide = held.shape[-1]
    half = lons // 2
    stride = 4 * rows + 1

    def one(pair, carry):
        both = []
        for side in range(2):
            block = grid_ref[pair * 2 + side]
            if wide > lats:
                block = jnp.concatenate([block, jnp.zeros((wide - lats, lons), block.dtype)], axis=0)
            both.append(block)
        stacked = jnp.concatenate(both, axis=0)
        low, high = stacked[:, :half], stacked[:, half:]
        for parity in range(2):
            folded = low + high if parity == 0 else low - high
            made = dot(table_ref[parity], folded, ((1,), (1,)))
            for side in range(2):
                for q in range(2):
                    piece = made[q * slots : (q + 1) * slots, side * wide : (side + 1) * wide]
                    start = parity * 2 * rows + q * rows + pair * 2 + side
                    held[pl.ds(start, slots, stride=stride), :] = piece * weight_ref[...]
        return carry

    lax.fori_loop(0, rows // 2, one, 0, unroll=2 if rows % 4 == 0 else 1)
    base = 0
    for out_ref in rest[:-1]:

        def put(slot, carry, base=base, out_ref=out_ref):
            value = held[pl.ds((base + slot) * stride, 4 * rows), :]
            out_ref[slot] = value.reshape(2, 2, rows, wide).astype(jnp.bfloat16)
            return carry

        lax.fori_loop(0, out_ref.shape[0], put, 0, unroll=2)
        base += out_ref.shape[0]


def fourier(grid_values, table, weight, counts, wide):
    rows, lats, lons = grid_values.shape
    slots = sum(counts)
    block = row_block(rows)
    return pl.pallas_call(
        fourier_kernel,
        grid=(rows // block,),
        in_specs=[
            pl.BlockSpec((block, lats, lons), lambda b: (b, 0, 0)),
            pl.BlockSpec(table.shape, lambda b: (0, 0, 0)),
            pl.BlockSpec(weight.shape, lambda b: (0, 0)),
        ],
        out_specs=[pl.BlockSpec((n, 2, 2, block, wide), lambda b: (0, 0, 0, b, 0)) for n in counts],
        out_shape=[jax.ShapeDtypeStruct((n, 2, 2, rows, wide), jnp.bfloat16) for n in counts],
        scratch_shapes=[pltpu.VMEM((slots * (4 * block + 1), wide), jnp.float32)],
        compiler_params=params(1),
        cost_estimate=cost(
            rows * lats * lons * slots * 4, rows * lats * lons * 2 + slots * rows * wide * 8
        ),
    )(grid_values, table, weight)


def basis_kernel(first_ref, basis_ref, lats_ref, out_ref):
    keep = out_ref.shape[1]
    size = (basis_ref.shape[1], out_ref.shape[2])
    hit = lax.broadcasted_iota(jnp.int32, size, 0) == lats_ref[0]
    order = jnp.where(hit, 1.0, 0.0).astype(jnp.bfloat16)
    for j in range(basis_ref.shape[0]):
        made = dot(basis_ref[j], order, ((0,), (0,)))
        out_ref[j] = made[:keep].astype(jnp.bfloat16)


def ordered_basis(basis, lats, keep, block, first, count, earlier):
    _, lat_count, columns = basis.shape
    wide = lats.shape[1]
    return pl.pallas_call(
        waiting(basis_kernel, 3, len(earlier)),
        grid_spec=pltpu.PrefetchScalarGridSpec(
            num_scalar_prefetch=1,
            grid=(count,),
            in_specs=[
                pl.BlockSpec((block, lat_count, columns), lambda i, first: (first[0] + i, 0, 0)),
                pl.BlockSpec((1, 1, wide), lambda i, first: (0, 0, 0)),
            ]
            + wait_specs(earlier),
            out_specs=pl.BlockSpec((block, keep, wide), lambda i, first: (i, 0, 0)),
        ),
        out_shape=jax.ShapeDtypeStruct((count * block, keep, wide), jnp.bfloat16),
        compiler_params=params(1),
        cost_estimate=cost(
            2 * count * block * lat_count * columns * wide,
            count * block * (lat_count * columns + keep * wide) * 2,
        ),
    )(first, basis, lats[:, None, :], *earlier)


def first_side(pair, waves, shape):
    column = lax.broadcasted_iota(jnp.int32, shape, 0)
    odd = pair & 1
    sign = 1 - 2 * odd
    return column * sign < (waves - pair) * sign + odd


def sums_of_pair(waves, pairs, values, bases):
    halves = []
    for j in range(2):
        made = dot(bases[j], values[j], ((1,), (1,)))
        width = made.shape[1] // 2
        side = first_side(pairs[j], waves, (made.shape[0], width))
        halves.append(jnp.where(side, made[:, :width], made[:, width:]))
    return jnp.concatenate(halves, axis=1)


def fields_of_pair(waves, pairs, coeff, bases):
    width = coeff.shape[1] // 2
    made = []
    for j in range(2):
        part = coeff[:, j * width : (j + 1) * width]
        side = first_side(pairs[j], waves, part.shape)
        empty = jnp.zeros_like(part)
        spread = jnp.concatenate(
            [jnp.where(side, part, empty), jnp.where(side, empty, part)], axis=1
        ).astype(jnp.bfloat16)
        made.append(dot(spread, bases[j], ((0,), (0,))).astype(jnp.bfloat16))
    return made


def sums_kernel(waves, base, blocks, pairs_ref, *rest):
    coeff_refs, basis_ref, out_ref = rest[:blocks], rest[blocks], rest[blocks + 1]
    parts = basis_ref.shape[1]
    start = base + pl.program_id(0) * parts
    for e in range(parts // 2):
        total = sums_of_pair(
            waves,
            [pairs_ref[start + 2 * e + j] for j in range(2)],
            [jnp.concatenate([ref[0, 2 * e + j] for ref in coeff_refs], axis=1) for j in range(2)],
            [basis_ref[0, 2 * e + j] for j in range(2)],
        )
        out_ref[0, e] = total.astype(jnp.bfloat16)


def fields_kernel(waves, base, pairs_ref, coeff_ref, basis_ref, *out_refs):
    parts, wide = basis_ref.shape[1], out_refs[0].shape[3]
    start = base + pl.program_id(0) * parts
    for e in range(parts // 2):
        made = fields_of_pair(
            waves,
            [pairs_ref[start + 2 * e + j] for j in range(2)],
            coeff_ref[0, e].astype(jnp.float32),
            [basis_ref[0, 2 * e + j] for j in range(2)],
        )
        for j in range(2):
            for u, ref in enumerate(out_refs):
                ref[0, 2 * e + j] = made[j][:, u * wide : (u + 1) * wide]


def legendre_call(
    kernel, scalars, operands, specs, shapes, out_specs, earlier, slots, keep, depth, wide
):
    steps = operands[0].shape[0]
    return pl.pallas_call(
        waiting(kernel, len(scalars) + len(operands), len(earlier)),
        grid_spec=pltpu.PrefetchScalarGridSpec(
            num_scalar_prefetch=len(scalars),
            grid=(steps,),
            in_specs=specs + wait_specs(earlier),
            out_specs=out_specs,
        ),
        out_shape=[jax.ShapeDtypeStruct(shape, jnp.bfloat16) for shape in shapes],
        compiler_params=params(1),
        cost_estimate=cost(
            4 * slots * keep * depth * wide, 4 * slots * (keep * wide + depth * wide)
        ),
    )(*scalars, *operands, *earlier)


def step_spec(shape, at):
    block = tuple(1 if d == at else size for d, size in enumerate(shape))
    return pl.BlockSpec(block, lambda i, *s: tuple(i if d == at else 0 for d in range(len(shape))))


def own_spec(basis, low):
    _, parts, keep, wide = basis.shape
    return pl.BlockSpec((1, parts, keep, wide), lambda i, *s: (low + i, 0, 0, 0))


def sums(waves, base, pairs, coeffs, basis, low, earlier):
    steps, parts, depth, wide = coeffs[0].shape
    keep = basis.shape[2]
    shape = (steps, parts // 2, keep, depth)
    return legendre_call(
        functools.partial(sums_kernel, waves, base, len(coeffs)),
        [pairs],
        [*coeffs, basis],
        [step_spec(x.shape, 0) for x in coeffs] + [own_spec(basis, low)],
        [shape],
        [step_spec(shape, 0)],
        earlier, steps * parts, keep, depth, wide * len(coeffs),
    )[0]


def fields(waves, base, pairs, coeff, basis, low, blocks, earlier):
    steps, half_parts, keep, depth = coeff.shape
    wide = basis.shape[3] // blocks
    shape = (steps, 2 * half_parts, depth, wide)
    return legendre_call(
        functools.partial(fields_kernel, waves, base),
        [pairs],
        [coeff, basis],
        [step_spec(coeff.shape, 0), own_spec(basis, low)],
        [shape] * blocks,
        [step_spec(shape, 0)] * blocks,
        earlier, steps * 2 * half_parts, keep, depth, wide * blocks,
    )


def matrices_kernel(lev_size, slot_ref, modes_in_ref, modes_out_ref, stiff_ref, in_ref, out_ref, row_ref):
    levels = modes_in_ref.shape[0]
    fields = in_ref.shape[2] // (4 * levels)
    rows = slot_ref.shape[0] // lev_size
    depth = 4 * rows
    lane = lax.broadcasted_iota(jnp.int32, (slot_ref.shape[0], levels), 1)
    hits = [slot_ref[...] - f * levels == lane for f in range(fields)]
    own = [jnp.where(hit, 1.0, 0.0).astype(jnp.bfloat16) for hit in hits]
    row_ref[...] = jnp.concatenate([stiff_ref[...]] * (4 * fields), axis=1)
    for target, modes, side in ((in_ref, modes_in_ref, 1), (out_ref, modes_out_ref, 0)):
        made = jnp.concatenate([dot(hit, modes[...], ((1,), (side,))) for hit in own], axis=1)
        empty = jnp.zeros((rows, made.shape[1]), jnp.float32)
        for v in range(lev_size):
            block = made[v * rows : (v + 1) * rows]
            lines = [
                jnp.concatenate([block if g == h else empty for h in range(4)], axis=1)
                for g in range(4)
            ]
            target[v] = jnp.concatenate(lines, axis=0).astype(jnp.bfloat16)


def matrices(field_slots, modes_in, modes_out, stiffness, lev_size):
    total, levels = field_slots.shape[0], modes_in.shape[0]
    shape = (lev_size, 4 * total // lev_size, 4 * total)
    return pl.pallas_call(
        functools.partial(matrices_kernel, lev_size),
        out_shape=[
            jax.ShapeDtypeStruct(shape, jnp.bfloat16),
            jax.ShapeDtypeStruct(shape, jnp.bfloat16),
            jax.ShapeDtypeStruct((1, 4 * total), jnp.float32),
        ],
        compiler_params=pltpu.CompilerParams(vmem_limit_bytes=VMEM_LIMIT),
        cost_estimate=cost(0, 4 * math.prod(shape)),
    )(field_slots[:, None], modes_in, modes_out, stiffness[None, :])


def solve_kernel(waves, base, keep, count, rank_ref, pairs_ref, arrived_ref, in_ref, out_of_ref, stiff_ref, out_ref):
    sources, share, _ = arrived_ref.shape
    total = dot(arrived_ref[0], in_ref[0], ((1,), (0,)))
    for source in range(1, sources):
        total = total + dot(arrived_ref[source], in_ref[source], ((1,), (0,)))
    width = total.shape[1] // 2
    place = rank_ref[0] * share + lax.broadcasted_iota(jnp.int32, (share, 1), 0)
    factors = []
    for j in range(2):
        column = place
        pair = jnp.zeros_like(place) + pairs_ref[base + j]
        for e in range(1, count):
            column = jnp.where(place >= e * keep, place - e * keep, column)
            pair = jnp.where(place >= e * keep, pairs_ref[base + 2 * e + j], pair)
        degree = jnp.where(column < waves - pair, pair + column, column - 1).astype(jnp.float32)
        growth = degree * (degree + 1.0) * (1.0 / (waves * waves))
        factors.append(1.0 / (1.0 + growth * stiff_ref[:, j * width : (j + 1) * width]))
    modal = (total * jnp.concatenate(factors, axis=1)).astype(jnp.bfloat16)
    for source in range(sources):
        out_ref[source] = dot(modal, out_of_ref[source], ((1,), (1,))).astype(jnp.bfloat16)


def solve(waves, base, keep, count, rank, pairs, arrived, into, out_of, stiff, earlier):
    def whole(shape):
        return pl.BlockSpec(shape, lambda i, *s: (0,) * len(shape))

    return pl.pallas_call(
        waiting(functools.partial(solve_kernel, waves, base, keep, count), 6, len(earlier)),
        grid_spec=pltpu.PrefetchScalarGridSpec(
            num_scalar_prefetch=2,
            grid=(1,),
            in_specs=[whole(x.shape) for x in (arrived, into, out_of, stiff)] + wait_specs(earlier),
            out_specs=whole(arrived.shape),
        ),
        out_shape=jax.ShapeDtypeStruct(arrived.shape, jnp.bfloat16),
        compiler_params=params(1),
        cost_estimate=cost(
            4 * arrived.size * into.shape[2], 2 * (arrived.size * 2 + into.size * 2)
        ),
    )(rank, pairs, arrived, into, out_of, stiff, *earlier)


def product_kernel(*refs):
    operands = refs[: len(refs) - 4]
    table_ref, grid_ref, out_ref, held = refs[len(refs) - 4 :]
    rows, lats, lons = grid_ref.shape
    wide = held.shape[-1]
    half = lons // 2
    stride = 4 * rows + 1
    slots = table_ref.shape[1] // 2
    base = 0
    for ref in operands:

        def take(d, carry, ref=ref, base=base):
            value = ref[d].astype(jnp.float32)
            held[pl.ds((base + d) * stride, 4 * rows), :] = value.reshape(4 * rows, wide)
            return carry

        lax.fori_loop(0, ref.shape[0], take, 0, unroll=2)
        base += ref.shape[0]

    def one(pair, carry):
        fields = []
        for parity in range(2):
            sides = []
            for side in range(2):
                start = parity * 2 * rows + pair * 2 + side
                sides.append(
                    jnp.concatenate(
                        [held[pl.ds(start + q * rows, slots, stride=stride), :] for q in range(2)],
                        axis=0,
                    ).astype(jnp.bfloat16)
                )
            fields.append(dot(jnp.concatenate(sides, axis=1), table_ref[parity], ((0,), (0,))))
        low, high = fields[0] + fields[1], fields[0] - fields[1]
        for side in range(2):
            row = pair * 2 + side
            block = grid_ref[row].astype(jnp.float32)
            out_ref[row, :, :half] = (
                low[side * wide : side * wide + lats] * block[:, :half]
            ).astype(jnp.bfloat16)
            out_ref[row, :, half:] = (
                high[side * wide : side * wide + lats] * block[:, half:]
            ).astype(jnp.bfloat16)
        return carry

    lax.fori_loop(0, rows // 2, one, 0)


def grid_product(operands, table, grid_values, wide):
    rows, lats, lons = grid_values.shape
    block = row_block(rows)
    slots = table.shape[1] // 2
    operands = [x.reshape(-1, 2, 2, rows, wide) for x in operands]
    grid_spec = pl.BlockSpec((block, lats, lons), lambda b: (b, 0, 0))
    return pl.pallas_call(
        product_kernel,
        grid=(rows // block,),
        in_specs=[
            pl.BlockSpec(x.shape[:3] + (block, wide), lambda b: (0, 0, 0, b, 0)) for x in operands
        ]
        + [pl.BlockSpec(table.shape, lambda b: (0, 0, 0)), grid_spec],
        out_specs=grid_spec,
        out_shape=jax.ShapeDtypeStruct(grid_values.shape, jnp.bfloat16),
        scratch_shapes=[pltpu.VMEM((slots * (4 * block + 1), wide), jnp.float32)],
        compiler_params=params(1),
        cost_estimate=cost(
            rows * lats * lons * slots * 4, rows * lats * lons * 4 + slots * rows * wide * 8
        ),
    )(*operands, table, grid_values)


PIECES = (3, 2)


def pieces_of(count):
    cuts, at = [], 0
    for size in PIECES:
        if at < count:
            cuts.append((at, min(count, at + size)))
            at += size
    if at < count:
        cuts.append((at, count))
    return cuts


def pick(table, rows):
    hit = rows[:, None] == jnp.arange(table.shape[0], dtype=jnp.int32)[None, :]
    hit = hit.reshape(hit.shape + (1,) * (table.ndim - 1))
    return jnp.sum(jnp.where(hit, table[None], 0), axis=1)


def local(
    grid_values,
    legendre,
    gauss_weights,
    modes_in,
    modes_out,
    stiffness,
    slot_pair,
    lat_order,
    field_slots,
):
    rows, lats, lons = grid_values.shape
    slots = legendre.shape[0]
    wave_size, lev_size = lax.axis_size("wave"), lax.axis_size("lev")
    wave_rank, lev_rank = lax.axis_index("wave"), lax.axis_index("lev")
    waves = 2 * slot_pair.shape[0]
    parts = math.gcd(slots, 8)
    chunks = slots // parts
    keep = round_up(waves + 1, 16)
    wide = round_up(lats, 128) if lats > 64 else round_up(lats, 32)
    depth = 4 * rows
    pieces = pieces_of(chunks)

    slot_at, owner_at = [], []
    for low, high in pieces:
        for u in range(wave_size):
            slot_at += range(low * parts, high * parts)
            owner_at += [u] * ((high - low) * parts)
    owner = wave_rank ^ jnp.array(owner_at, dtype=jnp.int32)
    pairs = pick(slot_pair, owner * slots + jnp.array(slot_at, dtype=jnp.int32))
    mirrored = waves - 1 - pairs
    odd_pair = (pairs & 1) == 1
    table = half_table(
        jnp.stack([jnp.where(odd_pair, mirrored, pairs), jnp.where(odd_pair, pairs, mirrored)]), lons
    )

    lat_blocks = jnp.pad(
        lat_order.reshape(wave_size, lats), ((0, 0), (0, wide - lats)), constant_values=-1
    )
    relative = wave_rank ^ jnp.arange(wave_size, dtype=jnp.int32)
    chosen = pick(lat_blocks, relative).reshape(1, -1)
    own_lats = pick(lat_blocks, wave_rank.reshape(1)).reshape(-1)
    row_weight = jnp.sum(
        jnp.where(
            own_lats[None, :] == jnp.arange(lat_order.shape[0], dtype=jnp.int32)[:, None],
            gauss_weights[:, None],
            0.0,
        ),
        axis=0,
        keepdims=True,
    )
    counts = [(high - low) * parts for low, high in pieces for _ in range(wave_size)]
    made = list(fourier(grid_values, table, row_weight, counts, wide))
    routes = [[(i, i ^ u) for i in range(wave_size)] for u in range(wave_size)]

    def exchange(blocks):
        return [blocks[0]] + [lax.ppermute(blocks[u], "wave", routes[u]) for u in range(1, wave_size)]

    coefficients = []
    for piece, (low, high) in enumerate(pieces):
        blocks = made[piece * wave_size : (piece + 1) * wave_size]
        shape = (high - low, parts, depth, wide)
        coefficients.append(exchange([block.reshape(shape) for block in blocks]))

    basis = ordered_basis(
        legendre, chosen, keep, chunks, jnp.zeros((1,), jnp.int32), parts, [made[0]]
    )
    basis = basis.reshape(chunks, parts, keep, -1)
    into, out_of, stiff = matrices(field_slots, modes_in, modes_out, stiffness, lev_size)
    rank = lev_rank.reshape(1)

    count = len(pieces)
    earlier = []
    arrived, returned, back = [None] * count, [None] * count, [None] * count

    def to_modes(piece):
        low, high = pieces[piece]
        flat = (high - low) * (parts // 2) * keep
        padded = round_up(flat, lev_size * 8)
        base = low * wave_size * parts
        spectral = sums(waves, base, pairs, coefficients[piece], basis, low, earlier)
        earlier[:] = [spectral]
        spectral = spectral.reshape(flat, depth)
        if padded > flat:
            spectral = jnp.pad(spectral, ((0, padded - flat), (0, 0)))
        arrived[piece] = lax.all_to_all(
            spectral.reshape(lev_size, -1, depth), "lev", split_axis=0, concat_axis=0, tiled=True
        )

    def solved(piece):
        low, high = pieces[piece]
        base = low * wave_size * parts
        held = (high - low) * (parts // 2)
        made = solve(
            waves, base, keep, held, rank, pairs, arrived[piece], into, out_of, stiff, earlier
        )
        earlier[:] = [made]
        returned[piece] = lax.all_to_all(made, "lev", split_axis=0, concat_axis=0, tiled=True)

    def to_waves(piece):
        low, high = pieces[piece]
        steps = high - low
        base = low * wave_size * parts
        implicit = returned[piece].reshape(-1, depth)[: steps * (parts // 2) * keep]
        implicit = implicit.reshape(steps, parts // 2, keep, depth)
        made = fields(waves, base, pairs, implicit, basis, low, wave_size, earlier)
        earlier[:] = [made[0]]
        back[piece] = exchange(made)

    to_modes(0)
    for piece in range(count):
        solved(piece)
        if piece + 1 < count:
            to_modes(piece + 1)
        if piece:
            earlier += back[piece - 1][1:]
        to_waves(piece)
    operands = [block for blocks in back for block in blocks]
    return grid_product(operands, table, grid_values, wide)


def solution(mesh):
    in_specs = (P("lev", "wave", None), P("wave", None, None), P(), P(), P(), P(), P(), P(), P())
    out_specs = P("lev", "wave", None)
    return jax.shard_map(local, mesh=mesh, in_specs=in_specs, out_specs=out_specs, check_vma=False)
```

```python
import functools
import math

import jax
import jax.numpy as jnp
from jax import lax
from jax.experimental import pallas as pl
from jax.experimental.pallas import tpu as pltpu
from jax.sharding import PartitionSpec as P

SCALE = 10.0
VMEM_LIMIT = 56 * 1024 * 1024


def round_up(value, unit):
    return -(-value // unit) * unit


def params(steps):
    return pltpu.CompilerParams(
        dimension_semantics=("arbitrary",) * steps, vmem_limit_bytes=VMEM_LIMIT
    )


def cost(flops, moved):
    return pl.CostEstimate(flops=int(flops * SCALE), bytes_accessed=int(moved * SCALE), transcendentals=0)


def waiting(kernel, inputs, count):
    def run(*refs):
        kernel(*refs[:inputs], *refs[inputs + count :])

    return run


def wait_specs(earlier):
    return [pl.BlockSpec(memory_space=pl.ANY)] * len(earlier)


def dot(left, right, dims):
    return lax.dot_general(left, right, (dims, ((), ())), preferred_element_type=jnp.float32)


def modulo(values, size):
    return values & (size - 1) if size & (size - 1) == 0 else lax.rem(values, size)


def half_table(wavenumbers, longitudes):
    lon = jnp.arange(longitudes // 2, dtype=jnp.int32)
    turn = jnp.arange(2, dtype=jnp.int32) * (longitudes // 4)
    steps = wavenumbers[:, None, :, None] * lon + turn[:, None, None]
    steps = modulo(steps, longitudes)
    eighth = longitudes // 8
    quarter = (
        (steps >= eighth).astype(jnp.int32)
        + (steps >= 3 * eighth).astype(jnp.int32)
        + (steps >= 5 * eighth).astype(jnp.int32)
        + (steps >= 7 * eighth).astype(jnp.int32)
    )
    angle = (steps - quarter * (2 * eighth)).astype(jnp.float32) * (2.0 * math.pi / longitudes)
    square = angle * angle
    cosine = 1.0 + square * (
        -0.5 + square * (1.0 / 24 + square * (-1.0 / 720 + square * (1.0 / 40320)))
    )
    sine = angle * (
        1.0 + square * (-1.0 / 6 + square * (1.0 / 120 + square * (-1.0 / 5040 + square / 362880)))
    )
    value = jnp.where((quarter & 1) == 0, cosine, sine)
    value = jnp.where((quarter == 1) | (quarter == 2), -value, value)
    scaled = value * (1.0 / math.sqrt(longitudes))
    return scaled.astype(jnp.bfloat16).reshape(2, -1, longitudes // 2)


def row_block(row_count):
    return 16 if row_count % 16 == 0 else row_count


def fourier_kernel(grid_ref, table_ref, weight_ref, *rest):
    held = rest[-1]
    rows, lats, lons = grid_ref.shape
    slots = table_ref.shape[1] // 2
    wide = held.shape[-1]
    half = lons // 2
    stride = 4 * rows + 1

    def one(pair, carry):
        both = []
        for side in range(2):
            block = grid_ref[pair * 2 + side]
            if wide > lats:
                block = jnp.concatenate([block, jnp.zeros((wide - lats, lons), block.dtype)], axis=0)
            both.append(block)
        stacked = jnp.concatenate(both, axis=0)
        low, high = stacked[:, :half], stacked[:, half:]
        for parity in range(2):
            folded = low + high if parity == 0 else low - high
            made = dot(table_ref[parity], folded, ((1,), (1,)))
            for side in range(2):
                for q in range(2):
                    piece = made[q * slots : (q + 1) * slots, side * wide : (side + 1) * wide]
                    start = parity * 2 * rows + q * rows + pair * 2 + side
                    held[pl.ds(start, slots, stride=stride), :] = piece * weight_ref[...]
        return carry

    lax.fori_loop(0, rows // 2, one, 0, unroll=2 if rows % 4 == 0 else 1)
    base = 0
    for out_ref in rest[:-1]:

        def put(slot, carry, base=base, out_ref=out_ref):
            value = held[pl.ds((base + slot) * stride, 4 * rows), :]
            out_ref[slot] = value.reshape(2, 2, rows, wide).astype(jnp.bfloat16)
            return carry

        lax.fori_loop(0, out_ref.shape[0], put, 0, unroll=2)
        base += out_ref.shape[0]


def fourier(grid_values, table, weight, counts, wide):
    rows, lats, lons = grid_values.shape
    slots = sum(counts)
    block = row_block(rows)
    return pl.pallas_call(
        fourier_kernel,
        grid=(rows // block,),
        in_specs=[
            pl.BlockSpec((block, lats, lons), lambda b: (b, 0, 0)),
            pl.BlockSpec(table.shape, lambda b: (0, 0, 0)),
            pl.BlockSpec(weight.shape, lambda b: (0, 0)),
        ],
        out_specs=[pl.BlockSpec((n, 2, 2, block, wide), lambda b: (0, 0, 0, b, 0)) for n in counts],
        out_shape=[jax.ShapeDtypeStruct((n, 2, 2, rows, wide), jnp.bfloat16) for n in counts],
        scratch_shapes=[pltpu.VMEM((slots * (4 * block + 1), wide), jnp.float32)],
        compiler_params=params(1),
        cost_estimate=cost(
            rows * lats * lons * slots * 4, rows * lats * lons * 2 + slots * rows * wide * 8
        ),
    )(grid_values, table, weight)


def basis_kernel(first_ref, basis_ref, lats_ref, out_ref):
    keep = out_ref.shape[1]
    size = (basis_ref.shape[1], out_ref.shape[2])
    hit = lax.broadcasted_iota(jnp.int32, size, 0) == lats_ref[0]
    order = jnp.where(hit, 1.0, 0.0).astype(jnp.bfloat16)
    for j in range(basis_ref.shape[0]):
        made = dot(basis_ref[j], order, ((0,), (0,)))
        out_ref[j] = made[:keep].astype(jnp.bfloat16)


def ordered_basis(basis, lats, keep, block, first, count, earlier):
    _, lat_count, columns = basis.shape
    wide = lats.shape[1]
    return pl.pallas_call(
        waiting(basis_kernel, 3, len(earlier)),
        grid_spec=pltpu.PrefetchScalarGridSpec(
            num_scalar_prefetch=1,
            grid=(count,),
            in_specs=[
                pl.BlockSpec((block, lat_count, columns), lambda i, first: (first[0] + i, 0, 0)),
                pl.BlockSpec((1, 1, wide), lambda i, first: (0, 0, 0)),
            ]
            + wait_specs(earlier),
            out_specs=pl.BlockSpec((block, keep, wide), lambda i, first: (i, 0, 0)),
        ),
        out_shape=jax.ShapeDtypeStruct((count * block, keep, wide), jnp.bfloat16),
        compiler_params=params(1),
        cost_estimate=cost(
            2 * count * block * lat_count * columns * wide,
            count * block * (lat_count * columns + keep * wide) * 2,
        ),
    )(first, basis, lats[:, None, :], *earlier)


def first_side(pair, waves, shape):
    column = lax.broadcasted_iota(jnp.int32, shape, 0)
    odd = pair & 1
    sign = 1 - 2 * odd
    return column * sign < (waves - pair) * sign + odd


def sums_of_pair(waves, pairs, values, bases):
    halves = []
    for j in range(2):
        made = dot(bases[j], values[j], ((1,), (1,)))
        width = made.shape[1] // 2
        side = first_side(pairs[j], waves, (made.shape[0], width))
        halves.append(jnp.where(side, made[:, :width], made[:, width:]))
    return jnp.concatenate(halves, axis=1)


def fields_of_pair(waves, pairs, coeff, bases):
    width = coeff.shape[1] // 2
    made = []
    for j in range(2):
        part = coeff[:, j * width : (j + 1) * width]
        side = first_side(pairs[j], waves, part.shape)
        empty = jnp.zeros_like(part)
        spread = jnp.concatenate(
            [jnp.where(side, part, empty), jnp.where(side, empty, part)], axis=1
        ).astype(jnp.bfloat16)
        made.append(dot(spread, bases[j], ((0,), (0,))).astype(jnp.bfloat16))
    return made


def sums_kernel(waves, base, blocks, pairs_ref, *rest):
    coeff_refs, basis_ref, out_ref = rest[:blocks], rest[blocks], rest[blocks + 1]
    parts = basis_ref.shape[1]
    start = base + pl.program_id(0) * parts
    for e in range(parts // 2):
        total = sums_of_pair(
            waves,
            [pairs_ref[start + 2 * e + j] for j in range(2)],
            [jnp.concatenate([ref[0, 2 * e + j] for ref in coeff_refs], axis=1) for j in range(2)],
            [basis_ref[0, 2 * e + j] for j in range(2)],
        )
        out_ref[0, e] = total.astype(jnp.bfloat16)


def fields_kernel(waves, base, pairs_ref, coeff_ref, basis_ref, *out_refs):
    parts, wide = basis_ref.shape[1], out_refs[0].shape[3]
    start = base + pl.program_id(0) * parts
    for e in range(parts // 2):
        made = fields_of_pair(
            waves,
            [pairs_ref[start + 2 * e + j] for j in range(2)],
            coeff_ref[0, e].astype(jnp.float32),
            [basis_ref[0, 2 * e + j] for j in range(2)],
        )
        for j in range(2):
            for u, ref in enumerate(out_refs):
                ref[0, 2 * e + j] = made[j][:, u * wide : (u + 1) * wide]


def legendre_call(
    kernel, scalars, operands, specs, shapes, out_specs, earlier, slots, keep, depth, wide
):
    steps = operands[0].shape[0]
    return pl.pallas_call(
        waiting(kernel, len(scalars) + len(operands), len(earlier)),
        grid_spec=pltpu.PrefetchScalarGridSpec(
            num_scalar_prefetch=len(scalars),
            grid=(steps,),
            in_specs=specs + wait_specs(earlier),
            out_specs=out_specs,
        ),
        out_shape=[jax.ShapeDtypeStruct(shape, jnp.bfloat16) for shape in shapes],
        compiler_params=params(1),
        cost_estimate=cost(
            4 * slots * keep * depth * wide, 4 * slots * (keep * wide + depth * wide)
        ),
    )(*scalars, *operands, *earlier)


def step_spec(shape, at):
    block = tuple(1 if d == at else size for d, size in enumerate(shape))
    return pl.BlockSpec(block, lambda i, *s: tuple(i if d == at else 0 for d in range(len(shape))))


def own_spec(basis, low):
    _, parts, keep, wide = basis.shape
    return pl.BlockSpec((1, parts, keep, wide), lambda i, *s: (low + i, 0, 0, 0))


def sums(waves, base, pairs, coeffs, basis, low, earlier):
    steps, parts, depth, wide = coeffs[0].shape
    keep = basis.shape[2]
    shape = (steps, parts // 2, keep, depth)
    return legendre_call(
        functools.partial(sums_kernel, waves, base, len(coeffs)),
        [pairs],
        [*coeffs, basis],
        [step_spec(x.shape, 0) for x in coeffs] + [own_spec(basis, low)],
        [shape],
        [step_spec(shape, 0)],
        earlier, steps * parts, keep, depth, wide * len(coeffs),
    )[0]


def fields(waves, base, pairs, coeff, basis, low, blocks, earlier):
    steps, half_parts, keep, depth = coeff.shape
    wide = basis.shape[3] // blocks
    shape = (steps, 2 * half_parts, depth, wide)
    return legendre_call(
        functools.partial(fields_kernel, waves, base),
        [pairs],
        [coeff, basis],
        [step_spec(coeff.shape, 0), own_spec(basis, low)],
        [shape] * blocks,
        [step_spec(shape, 0)] * blocks,
        earlier, steps * 2 * half_parts, keep, depth, wide * blocks,
    )


def matrices_kernel(lev_size, slot_ref, modes_in_ref, modes_out_ref, stiff_ref, in_ref, out_ref, row_ref):
    levels = modes_in_ref.shape[0]
    fields = in_ref.shape[2] // (4 * levels)
    rows = slot_ref.shape[0] // lev_size
    depth = 4 * rows
    lane = lax.broadcasted_iota(jnp.int32, (slot_ref.shape[0], levels), 1)
    hits = [slot_ref[...] - f * levels == lane for f in range(fields)]
    own = [jnp.where(hit, 1.0, 0.0).astype(jnp.bfloat16) for hit in hits]
    row_ref[...] = jnp.concatenate([stiff_ref[...]] * (4 * fields), axis=1)
    for target, modes, side in ((in_ref, modes_in_ref, 1), (out_ref, modes_out_ref, 0)):
        made = jnp.concatenate([dot(hit, modes[...], ((1,), (side,))) for hit in own], axis=1)
        empty = jnp.zeros((rows, made.shape[1]), jnp.float32)
        for v in range(lev_size):
            block = made[v * rows : (v + 1) * rows]
            lines = [
                jnp.concatenate([block if g == h else empty for h in range(4)], axis=1)
                for g in range(4)
            ]
            target[v] = jnp.concatenate(lines, axis=0).astype(jnp.bfloat16)


def matrices(field_slots, modes_in, modes_out, stiffness, lev_size):
    total, levels = field_slots.shape[0], modes_in.shape[0]
    shape = (lev_size, 4 * total // lev_size, 4 * total)
    return pl.pallas_call(
        functools.partial(matrices_kernel, lev_size),
        out_shape=[
            jax.ShapeDtypeStruct(shape, jnp.bfloat16),
            jax.ShapeDtypeStruct(shape, jnp.bfloat16),
            jax.ShapeDtypeStruct((1, 4 * total), jnp.float32),
        ],
        compiler_params=pltpu.CompilerParams(vmem_limit_bytes=VMEM_LIMIT),
        cost_estimate=cost(0, 4 * math.prod(shape)),
    )(field_slots[:, None], modes_in, modes_out, stiffness[None, :])


def solve_kernel(waves, base, keep, count, rank_ref, pairs_ref, arrived_ref, in_ref, out_of_ref, stiff_ref, out_ref):
    sources, share, _ = arrived_ref.shape
    total = dot(arrived_ref[0], in_ref[0], ((1,), (0,)))
    for source in range(1, sources):
        total = total + dot(arrived_ref[source], in_ref[source], ((1,), (0,)))
    width = total.shape[1] // 2
    place = rank_ref[0] * share + lax.broadcasted_iota(jnp.int32, (share, 1), 0)
    factors = []
    for j in range(2):
        column = place
        pair = jnp.zeros_like(place) + pairs_ref[base + j]
        for e in range(1, count):
            column = jnp.where(place >= e * keep, place - e * keep, column)
            pair = jnp.where(place >= e * keep, pairs_ref[base + 2 * e + j], pair)
        degree = jnp.where(column < waves - pair, pair + column, column - 1).astype(jnp.float32)
        growth = degree * (degree + 1.0) * (1.0 / (waves * waves))
        factors.append(1.0 / (1.0 + growth * stiff_ref[:, j * width : (j + 1) * width]))
    modal = (total * jnp.concatenate(factors, axis=1)).astype(jnp.bfloat16)
    for source in range(sources):
        out_ref[source] = dot(modal, out_of_ref[source], ((1,), (1,))).astype(jnp.bfloat16)


def solve(waves, base, keep, count, rank, pairs, arrived, into, out_of, stiff, earlier):
    def whole(shape):
        return pl.BlockSpec(shape, lambda i, *s: (0,) * len(shape))

    return pl.pallas_call(
        waiting(functools.partial(solve_kernel, waves, base, keep, count), 6, len(earlier)),
        grid_spec=pltpu.PrefetchScalarGridSpec(
            num_scalar_prefetch=2,
            grid=(1,),
            in_specs=[whole(x.shape) for x in (arrived, into, out_of, stiff)] + wait_specs(earlier),
            out_specs=whole(arrived.shape),
        ),
        out_shape=jax.ShapeDtypeStruct(arrived.shape, jnp.bfloat16),
        compiler_params=params(1),
        cost_estimate=cost(
            4 * arrived.size * into.shape[2], 2 * (arrived.size * 2 + into.size * 2)
        ),
    )(rank, pairs, arrived, into, out_of, stiff, *earlier)


def product_kernel(*refs):
    operands = refs[: len(refs) - 4]
    table_ref, grid_ref, out_ref, held = refs[len(refs) - 4 :]
    rows, lats, lons = grid_ref.shape
    wide = held.shape[-1]
    half = lons // 2
    stride = 4 * rows + 1
    slots = table_ref.shape[1] // 2
    base = 0
    for ref in operands:

        def take(d, carry, ref=ref, base=base):
            value = ref[d].astype(jnp.float32)
            held[pl.ds((base + d) * stride, 4 * rows), :] = value.reshape(4 * rows, wide)
            return carry

        lax.fori_loop(0, ref.shape[0], take, 0, unroll=2)
        base += ref.shape[0]

    def one(pair, carry):
        fields = []
        for parity in range(2):
            sides = []
            for side in range(2):
                start = parity * 2 * rows + pair * 2 + side
                sides.append(
                    jnp.concatenate(
                        [held[pl.ds(start + q * rows, slots, stride=stride), :] for q in range(2)],
                        axis=0,
                    ).astype(jnp.bfloat16)
                )
            fields.append(dot(jnp.concatenate(sides, axis=1), table_ref[parity], ((0,), (0,))))
        low, high = fields[0] + fields[1], fields[0] - fields[1]
        for side in range(2):
            row = pair * 2 + side
            block = grid_ref[row].astype(jnp.float32)
            out_ref[row, :, :half] = (
                low[side * wide : side * wide + lats] * block[:, :half]
            ).astype(jnp.bfloat16)
            out_ref[row, :, half:] = (
                high[side * wide : side * wide + lats] * block[:, half:]
            ).astype(jnp.bfloat16)
        return carry

    lax.fori_loop(0, rows // 2, one, 0)


def grid_product(operands, table, grid_values, wide):
    rows, lats, lons = grid_values.shape
    block = row_block(rows)
    slots = table.shape[1] // 2
    operands = [x.reshape(-1, 2, 2, rows, wide) for x in operands]
    grid_spec = pl.BlockSpec((block, lats, lons), lambda b: (b, 0, 0))
    return pl.pallas_call(
        product_kernel,
        grid=(rows // block,),
        in_specs=[
            pl.BlockSpec(x.shape[:3] + (block, wide), lambda b: (0, 0, 0, b, 0)) for x in operands
        ]
        + [pl.BlockSpec(table.shape, lambda b: (0, 0, 0)), grid_spec],
        out_specs=grid_spec,
        out_shape=jax.ShapeDtypeStruct(grid_values.shape, jnp.bfloat16),
        scratch_shapes=[pltpu.VMEM((slots * (4 * block + 1), wide), jnp.float32)],
        compiler_params=params(1),
        cost_estimate=cost(
            rows * lats * lons * slots * 4, rows * lats * lons * 4 + slots * rows * wide * 8
        ),
    )(*operands, table, grid_values)


PIECES = (3, 2)


def pieces_of(count):
    cuts, at = [], 0
    for size in PIECES:
        if at < count:
            cuts.append((at, min(count, at + size)))
            at += size
    if at < count:
        cuts.append((at, count))
    return cuts


def pick(table, rows):
    hit = rows[:, None] == jnp.arange(table.shape[0], dtype=jnp.int32)[None, :]
    hit = hit.reshape(hit.shape + (1,) * (table.ndim - 1))
    return jnp.sum(jnp.where(hit, table[None], 0), axis=1)


def local(
    grid_values,
    legendre,
    gauss_weights,
    modes_in,
    modes_out,
    stiffness,
    slot_pair,
    lat_order,
    field_slots,
):
    rows, lats, lons = grid_values.shape
    slots = legendre.shape[0]
    wave_size, lev_size = lax.axis_size("wave"), lax.axis_size("lev")
    wave_rank, lev_rank = lax.axis_index("wave"), lax.axis_index("lev")
    waves = 2 * slot_pair.shape[0]
    parts = math.gcd(slots, 8)
    chunks = slots // parts
    keep = round_up(waves + 1, 16)
    wide = round_up(lats, 128) if lats > 64 else round_up(lats, 32)
    depth = 4 * rows
    pieces = pieces_of(chunks)

    slot_at, owner_at = [], []
    for low, high in pieces:
        for u in range(wave_size):
            slot_at += range(low * parts, high * parts)
            owner_at += [u] * ((high - low) * parts)
    owner = wave_rank ^ jnp.array(owner_at, dtype=jnp.int32)
    pairs = pick(slot_pair, owner * slots + jnp.array(slot_at, dtype=jnp.int32))
    mirrored = waves - 1 - pairs
    odd_pair = (pairs & 1) == 1
    table = half_table(
        jnp.stack([jnp.where(odd_pair, mirrored, pairs), jnp.where(odd_pair, pairs, mirrored)]), lons
    )

    lat_blocks = jnp.pad(
        lat_order.reshape(wave_size, lats), ((0, 0), (0, wide - lats)), constant_values=-1
    )
    relative = wave_rank ^ jnp.arange(wave_size, dtype=jnp.int32)
    chosen = pick(lat_blocks, relative).reshape(1, -1)
    own_lats = pick(lat_blocks, wave_rank.reshape(1)).reshape(-1)
    row_weight = jnp.sum(
        jnp.where(
            own_lats[None, :] == jnp.arange(lat_order.shape[0], dtype=jnp.int32)[:, None],
            gauss_weights[:, None],
            0.0,
        ),
        axis=0,
        keepdims=True,
    )
    counts = [(high - low) * parts for low, high in pieces for _ in range(wave_size)]
    made = list(fourier(grid_values, table, row_weight, counts, wide))
    routes = [[(i, i ^ u) for i in range(wave_size)] for u in range(wave_size)]

    def exchange(blocks):
        return [blocks[0]] + [lax.ppermute(blocks[u], "wave", routes[u]) for u in range(1, wave_size)]

    coefficients = []
    for piece, (low, high) in enumerate(pieces):
        blocks = made[piece * wave_size : (piece + 1) * wave_size]
        shape = (high - low, parts, depth, wide)
        coefficients.append(exchange([block.reshape(shape) for block in blocks]))

    basis = ordered_basis(
        legendre, chosen, keep, chunks, jnp.zeros((1,), jnp.int32), parts, [made[0]]
    )
    basis = basis.reshape(chunks, parts, keep, -1)
    into, out_of, stiff = matrices(field_slots, modes_in, modes_out, stiffness, lev_size)
    rank = lev_rank.reshape(1)

    count = len(pieces)
    earlier = []
    arrived, returned, back = [None] * count, [None] * count, [None] * count

    def to_modes(piece):
        low, high = pieces[piece]
        flat = (high - low) * (parts // 2) * keep
        padded = round_up(flat, lev_size * 8)
        base = low * wave_size * parts
        spectral = sums(waves, base, pairs, coefficients[piece], basis, low, earlier)
        earlier[:] = [spectral]
        spectral = spectral.reshape(flat, depth)
        if padded > flat:
            spectral = jnp.pad(spectral, ((0, padded - flat), (0, 0)))
        arrived[piece] = lax.all_to_all(
            spectral.reshape(lev_size, -1, depth), "lev", split_axis=0, concat_axis=0, tiled=True
        )

    def solved(piece):
        low, high = pieces[piece]
        base = low * wave_size * parts
        held = (high - low) * (parts // 2)
        made = solve(
            waves, base, keep, held, rank, pairs, arrived[piece], into, out_of, stiff, earlier
        )
        earlier[:] = [made]
        returned[piece] = lax.all_to_all(made, "lev", split_axis=0, concat_axis=0, tiled=True)

    def to_waves(piece):
        low, high = pieces[piece]
        steps = high - low
        base = low * wave_size * parts
        implicit = returned[piece].reshape(-1, depth)[: steps * (parts // 2) * keep]
        implicit = implicit.reshape(steps, parts // 2, keep, depth)
        made = fields(waves, base, pairs, implicit, basis, low, wave_size, earlier)
        earlier[:] = [made[0]]
        back[piece] = exchange(made)

    to_modes(0)
    for piece in range(count):
        solved(piece)
        if piece + 1 < count:
            to_modes(piece + 1)
        if piece:
            earlier += back[piece - 1][1:-1]
        to_waves(piece)
    operands = [block for blocks in back for block in blocks]
    return grid_product(operands, table, grid_values, wide)


def solution(mesh):
    in_specs = (P("lev", "wave", None), P("wave", None, None), P(), P(), P(), P(), P(), P(), P())
    out_specs = P("lev", "wave", None)
    return jax.shard_map(local, mesh=mesh, in_specs=in_specs, out_specs=out_specs, check_vma=False)
```

```python
import functools
import math

import jax
import jax.numpy as jnp
from jax import lax
from jax.experimental import pallas as pl
from jax.experimental.pallas import tpu as pltpu
from jax.sharding import PartitionSpec as P

SCALE = 10.0
VMEM_LIMIT = 56 * 1024 * 1024


def round_up(value, unit):
    return -(-value // unit) * unit


def params(steps):
    return pltpu.CompilerParams(
        dimension_semantics=("arbitrary",) * steps, vmem_limit_bytes=VMEM_LIMIT
    )


def cost(flops, moved):
    return pl.CostEstimate(flops=int(flops * SCALE), bytes_accessed=int(moved * SCALE), transcendentals=0)


def waiting(kernel, inputs, count):
    def run(*refs):
        kernel(*refs[:inputs], *refs[inputs + count :])

    return run


def wait_specs(earlier):
    return [pl.BlockSpec(memory_space=pl.ANY)] * len(earlier)


def dot(left, right, dims):
    return lax.dot_general(left, right, (dims, ((), ())), preferred_element_type=jnp.float32)


def modulo(values, size):
    return values & (size - 1) if size & (size - 1) == 0 else lax.rem(values, size)


def half_table(wavenumbers, longitudes):
    lon = jnp.arange(longitudes // 2, dtype=jnp.int32)
    turn = jnp.arange(2, dtype=jnp.int32) * (longitudes // 4)
    steps = wavenumbers[:, None, :, None] * lon + turn[:, None, None]
    steps = modulo(steps, longitudes)
    eighth = longitudes // 8
    quarter = (
        (steps >= eighth).astype(jnp.int32)
        + (steps >= 3 * eighth).astype(jnp.int32)
        + (steps >= 5 * eighth).astype(jnp.int32)
        + (steps >= 7 * eighth).astype(jnp.int32)
    )
    angle = (steps - quarter * (2 * eighth)).astype(jnp.float32) * (2.0 * math.pi / longitudes)
    square = angle * angle
    cosine = 1.0 + square * (
        -0.5 + square * (1.0 / 24 + square * (-1.0 / 720 + square * (1.0 / 40320)))
    )
    sine = angle * (
        1.0 + square * (-1.0 / 6 + square * (1.0 / 120 + square * (-1.0 / 5040 + square / 362880)))
    )
    value = jnp.where((quarter & 1) == 0, cosine, sine)
    value = jnp.where((quarter == 1) | (quarter == 2), -value, value)
    scaled = value * (1.0 / math.sqrt(longitudes))
    return scaled.astype(jnp.bfloat16).reshape(2, -1, longitudes // 2)


def row_block(row_count):
    return 16 if row_count % 16 == 0 else row_count


def fourier_kernel(grid_ref, table_ref, weight_ref, *rest):
    held = rest[-1]
    rows, lats, lons = grid_ref.shape
    slots = table_ref.shape[1] // 2
    wide = held.shape[-1]
    half = lons // 2
    stride = 4 * rows + 1

    def one(pair, carry):
        both = []
        for side in range(2):
            block = grid_ref[pair * 2 + side]
            if wide > lats:
                block = jnp.concatenate([block, jnp.zeros((wide - lats, lons), block.dtype)], axis=0)
            both.append(block)
        stacked = jnp.concatenate(both, axis=0)
        low, high = stacked[:, :half], stacked[:, half:]
        for parity in range(2):
            folded = low + high if parity == 0 else low - high
            made = dot(table_ref[parity], folded, ((1,), (1,)))
            for side in range(2):
                for q in range(2):
                    piece = made[q * slots : (q + 1) * slots, side * wide : (side + 1) * wide]
                    start = parity * 2 * rows + q * rows + pair * 2 + side
                    held[pl.ds(start, slots, stride=stride), :] = piece * weight_ref[...]
        return carry

    lax.fori_loop(0, rows // 2, one, 0, unroll=2 if rows % 4 == 0 else 1)
    base = 0
    for out_ref in rest[:-1]:

        def put(slot, carry, base=base, out_ref=out_ref):
            value = held[pl.ds((base + slot) * stride, 4 * rows), :]
            out_ref[slot] = value.reshape(2, 2, rows, wide).astype(jnp.bfloat16)
            return carry

        lax.fori_loop(0, out_ref.shape[0], put, 0, unroll=2)
        base += out_ref.shape[0]


def fourier(grid_values, table, weight, counts, wide):
    rows, lats, lons = grid_values.shape
    slots = sum(counts)
    block = row_block(rows)
    return pl.pallas_call(
        fourier_kernel,
        grid=(rows // block,),
        in_specs=[
            pl.BlockSpec((block, lats, lons), lambda b: (b, 0, 0)),
            pl.BlockSpec(table.shape, lambda b: (0, 0, 0)),
            pl.BlockSpec(weight.shape, lambda b: (0, 0)),
        ],
        out_specs=[pl.BlockSpec((n, 2, 2, block, wide), lambda b: (0, 0, 0, b, 0)) for n in counts],
        out_shape=[jax.ShapeDtypeStruct((n, 2, 2, rows, wide), jnp.bfloat16) for n in counts],
        scratch_shapes=[pltpu.VMEM((slots * (4 * block + 1), wide), jnp.float32)],
        compiler_params=params(1),
        cost_estimate=cost(
            rows * lats * lons * slots * 4, rows * lats * lons * 2 + slots * rows * wide * 8
        ),
    )(grid_values, table, weight)


def basis_kernel(first_ref, basis_ref, lats_ref, out_ref):
    keep = out_ref.shape[1]
    size = (basis_ref.shape[1], out_ref.shape[2])
    hit = lax.broadcasted_iota(jnp.int32, size, 0) == lats_ref[0]
    order = jnp.where(hit, 1.0, 0.0).astype(jnp.bfloat16)
    for j in range(basis_ref.shape[0]):
        made = dot(basis_ref[j], order, ((0,), (0,)))
        out_ref[j] = made[:keep].astype(jnp.bfloat16)


def ordered_basis(basis, lats, keep, block, first, count, earlier):
    _, lat_count, columns = basis.shape
    wide = lats.shape[1]
    return pl.pallas_call(
        waiting(basis_kernel, 3, len(earlier)),
        grid_spec=pltpu.PrefetchScalarGridSpec(
            num_scalar_prefetch=1,
            grid=(count,),
            in_specs=[
                pl.BlockSpec((block, lat_count, columns), lambda i, first: (first[0] + i, 0, 0)),
                pl.BlockSpec((1, 1, wide), lambda i, first: (0, 0, 0)),
            ]
            + wait_specs(earlier),
            out_specs=pl.BlockSpec((block, keep, wide), lambda i, first: (i, 0, 0)),
        ),
        out_shape=jax.ShapeDtypeStruct((count * block, keep, wide), jnp.bfloat16),
        compiler_params=params(1),
        cost_estimate=cost(
            2 * count * block * lat_count * columns * wide,
            count * block * (lat_count * columns + keep * wide) * 2,
        ),
    )(first, basis, lats[:, None, :], *earlier)


def first_side(pair, waves, shape):
    column = lax.broadcasted_iota(jnp.int32, shape, 0)
    odd = pair & 1
    sign = 1 - 2 * odd
    return column * sign < (waves - pair) * sign + odd


def sums_of_pair(waves, pairs, values, bases):
    halves = []
    for j in range(2):
        made = dot(bases[j], values[j], ((1,), (1,)))
        width = made.shape[1] // 2
        side = first_side(pairs[j], waves, (made.shape[0], width))
        halves.append(jnp.where(side, made[:, :width], made[:, width:]))
    return jnp.concatenate(halves, axis=1)


def fields_of_pair(waves, pairs, coeff, bases):
    width = coeff.shape[1] // 2
    made = []
    for j in range(2):
        part = coeff[:, j * width : (j + 1) * width]
        side = first_side(pairs[j], waves, part.shape)
        empty = jnp.zeros_like(part)
        spread = jnp.concatenate(
            [jnp.where(side, part, empty), jnp.where(side, empty, part)], axis=1
        ).astype(jnp.bfloat16)
        made.append(dot(spread, bases[j], ((0,), (0,))).astype(jnp.bfloat16))
    return made


def sums_kernel(waves, base, blocks, pairs_ref, *rest):
    coeff_refs, basis_ref, out_ref = rest[:blocks], rest[blocks], rest[blocks + 1]
    parts = basis_ref.shape[1]
    start = base + pl.program_id(0) * parts
    for e in range(parts // 2):
        total = sums_of_pair(
            waves,
            [pairs_ref[start + 2 * e + j] for j in range(2)],
            [jnp.concatenate([ref[0, 2 * e + j] for ref in coeff_refs], axis=1) for j in range(2)],
            [basis_ref[0, 2 * e + j] for j in range(2)],
        )
        out_ref[0, e] = total.astype(jnp.bfloat16)


def fields_kernel(waves, base, pairs_ref, coeff_ref, basis_ref, *out_refs):
    parts, wide = basis_ref.shape[1], out_refs[0].shape[3]
    start = base + pl.program_id(0) * parts
    for e in range(parts // 2):
        made = fields_of_pair(
            waves,
            [pairs_ref[start + 2 * e + j] for j in range(2)],
            coeff_ref[0, e].astype(jnp.float32),
            [basis_ref[0, 2 * e + j] for j in range(2)],
        )
        for j in range(2):
            for u, ref in enumerate(out_refs):
                ref[0, 2 * e + j] = made[j][:, u * wide : (u + 1) * wide]


def legendre_call(
    kernel, scalars, operands, specs, shapes, out_specs, earlier, slots, keep, depth, wide
):
    steps = operands[0].shape[0]
    return pl.pallas_call(
        waiting(kernel, len(scalars) + len(operands), len(earlier)),
        grid_spec=pltpu.PrefetchScalarGridSpec(
            num_scalar_prefetch=len(scalars),
            grid=(steps,),
            in_specs=specs + wait_specs(earlier),
            out_specs=out_specs,
        ),
        out_shape=[jax.ShapeDtypeStruct(shape, jnp.bfloat16) for shape in shapes],
        compiler_params=params(1),
        cost_estimate=cost(
            4 * slots * keep * depth * wide, 4 * slots * (keep * wide + depth * wide)
        ),
    )(*scalars, *operands, *earlier)


def step_spec(shape, at):
    block = tuple(1 if d == at else size for d, size in enumerate(shape))
    return pl.BlockSpec(block, lambda i, *s: tuple(i if d == at else 0 for d in range(len(shape))))


def own_spec(basis, low):
    _, parts, keep, wide = basis.shape
    return pl.BlockSpec((1, parts, keep, wide), lambda i, *s: (low + i, 0, 0, 0))


def sums(waves, base, pairs, coeffs, basis, low, earlier):
    steps, parts, depth, wide = coeffs[0].shape
    keep = basis.shape[2]
    shape = (steps, parts // 2, keep, depth)
    return legendre_call(
        functools.partial(sums_kernel, waves, base, len(coeffs)),
        [pairs],
        [*coeffs, basis],
        [step_spec(x.shape, 0) for x in coeffs] + [own_spec(basis, low)],
        [shape],
        [step_spec(shape, 0)],
        earlier, steps * parts, keep, depth, wide * len(coeffs),
    )[0]


def fields(waves, base, pairs, coeff, basis, low, blocks, earlier):
    steps, half_parts, keep, depth = coeff.shape
    wide = basis.shape[3] // blocks
    shape = (steps, 2 * half_parts, depth, wide)
    return legendre_call(
        functools.partial(fields_kernel, waves, base),
        [pairs],
        [coeff, basis],
        [step_spec(coeff.shape, 0), own_spec(basis, low)],
        [shape] * blocks,
        [step_spec(shape, 0)] * blocks,
        earlier, steps * 2 * half_parts, keep, depth, wide * blocks,
    )


def matrices_kernel(lev_size, slot_ref, modes_in_ref, modes_out_ref, stiff_ref, in_ref, out_ref, row_ref):
    levels = modes_in_ref.shape[0]
    fields = in_ref.shape[2] // (4 * levels)
    rows = slot_ref.shape[0] // lev_size
    depth = 4 * rows
    lane = lax.broadcasted_iota(jnp.int32, (slot_ref.shape[0], levels), 1)
    hits = [slot_ref[...] - f * levels == lane for f in range(fields)]
    own = [jnp.where(hit, 1.0, 0.0).astype(jnp.bfloat16) for hit in hits]
    row_ref[...] = jnp.concatenate([stiff_ref[...]] * (4 * fields), axis=1)
    for target, modes, side in ((in_ref, modes_in_ref, 1), (out_ref, modes_out_ref, 0)):
        made = jnp.concatenate([dot(hit, modes[...], ((1,), (side,))) for hit in own], axis=1)
        empty = jnp.zeros((rows, made.shape[1]), jnp.float32)
        for v in range(lev_size):
            block = made[v * rows : (v + 1) * rows]
            lines = [
                jnp.concatenate([block if g == h else empty for h in range(4)], axis=1)
                for g in range(4)
            ]
            target[v] = jnp.concatenate(lines, axis=0).astype(jnp.bfloat16)


def matrices(field_slots, modes_in, modes_out, stiffness, lev_size):
    total, levels = field_slots.shape[0], modes_in.shape[0]
    shape = (lev_size, 4 * total // lev_size, 4 * total)
    return pl.pallas_call(
        functools.partial(matrices_kernel, lev_size),
        out_shape=[
            jax.ShapeDtypeStruct(shape, jnp.bfloat16),
            jax.ShapeDtypeStruct(shape, jnp.bfloat16),
            jax.ShapeDtypeStruct((1, 4 * total), jnp.float32),
        ],
        compiler_params=pltpu.CompilerParams(vmem_limit_bytes=VMEM_LIMIT),
        cost_estimate=cost(0, 4 * math.prod(shape)),
    )(field_slots[:, None], modes_in, modes_out, stiffness[None, :])


def solve_kernel(waves, base, keep, count, rank_ref, pairs_ref, arrived_ref, in_ref, out_of_ref, stiff_ref, out_ref):
    sources, share, _ = arrived_ref.shape
    total = dot(arrived_ref[0], in_ref[0], ((1,), (0,)))
    for source in range(1, sources):
        total = total + dot(arrived_ref[source], in_ref[source], ((1,), (0,)))
    width = total.shape[1] // 2
    place = rank_ref[0] * share + lax.broadcasted_iota(jnp.int32, (share, 1), 0)
    factors = []
    for j in range(2):
        column = place
        pair = jnp.zeros_like(place) + pairs_ref[base + j]
        for e in range(1, count):
            column = jnp.where(place >= e * keep, place - e * keep, column)
            pair = jnp.where(place >= e * keep, pairs_ref[base + 2 * e + j], pair)
        degree = jnp.where(column < waves - pair, pair + column, column - 1).astype(jnp.float32)
        growth = degree * (degree + 1.0) * (1.0 / (waves * waves))
        factors.append(1.0 / (1.0 + growth * stiff_ref[:, j * width : (j + 1) * width]))
    modal = (total * jnp.concatenate(factors, axis=1)).astype(jnp.bfloat16)
    for source in range(sources):
        out_ref[source] = dot(modal, out_of_ref[source], ((1,), (1,))).astype(jnp.bfloat16)


def solve(waves, base, keep, count, rank, pairs, arrived, into, out_of, stiff, earlier):
    def whole(shape):
        return pl.BlockSpec(shape, lambda i, *s: (0,) * len(shape))

    return pl.pallas_call(
        waiting(functools.partial(solve_kernel, waves, base, keep, count), 6, len(earlier)),
        grid_spec=pltpu.PrefetchScalarGridSpec(
            num_scalar_prefetch=2,
            grid=(1,),
            in_specs=[whole(x.shape) for x in (arrived, into, out_of, stiff)] + wait_specs(earlier),
            out_specs=whole(arrived.shape),
        ),
        out_shape=jax.ShapeDtypeStruct(arrived.shape, jnp.bfloat16),
        compiler_params=params(1),
        cost_estimate=cost(
            4 * arrived.size * into.shape[2], 2 * (arrived.size * 2 + into.size * 2)
        ),
    )(rank, pairs, arrived, into, out_of, stiff, *earlier)


def product_kernel(*refs):
    operands = refs[: len(refs) - 4]
    table_ref, grid_ref, out_ref, held = refs[len(refs) - 4 :]
    rows, lats, lons = grid_ref.shape
    wide = held.shape[-1]
    half = lons // 2
    stride = 4 * rows + 1
    slots = table_ref.shape[1] // 2
    base = 0
    for ref in operands:

        def take(d, carry, ref=ref, base=base):
            value = ref[d].astype(jnp.float32)
            held[pl.ds((base + d) * stride, 4 * rows), :] = value.reshape(4 * rows, wide)
            return carry

        lax.fori_loop(0, ref.shape[0], take, 0, unroll=4)
        base += ref.shape[0]

    def one(pair, carry):
        fields = []
        for parity in range(2):
            sides = []
            for side in range(2):
                start = parity * 2 * rows + pair * 2 + side
                sides.append(
                    jnp.concatenate(
                        [held[pl.ds(start + q * rows, slots, stride=stride), :] for q in range(2)],
                        axis=0,
                    ).astype(jnp.bfloat16)
                )
            fields.append(dot(jnp.concatenate(sides, axis=1), table_ref[parity], ((0,), (0,))))
        low, high = fields[0] + fields[1], fields[0] - fields[1]
        for side in range(2):
            row = pair * 2 + side
            block = grid_ref[row].astype(jnp.float32)
            out_ref[row, :, :half] = (
                low[side * wide : side * wide + lats] * block[:, :half]
            ).astype(jnp.bfloat16)
            out_ref[row, :, half:] = (
                high[side * wide : side * wide + lats] * block[:, half:]
            ).astype(jnp.bfloat16)
        return carry

    lax.fori_loop(0, rows // 2, one, 0, unroll=2 if rows % 4 == 0 else 1)


def grid_product(operands, table, grid_values, wide):
    rows, lats, lons = grid_values.shape
    block = row_block(rows)
    slots = table.shape[1] // 2
    operands = [x.reshape(-1, 2, 2, rows, wide) for x in operands]
    grid_spec = pl.BlockSpec((block, lats, lons), lambda b: (b, 0, 0))
    return pl.pallas_call(
        product_kernel,
        grid=(rows // block,),
        in_specs=[
            pl.BlockSpec(x.shape[:3] + (block, wide), lambda b: (0, 0, 0, b, 0)) for x in operands
        ]
        + [pl.BlockSpec(table.shape, lambda b: (0, 0, 0)), grid_spec],
        out_specs=grid_spec,
        out_shape=jax.ShapeDtypeStruct(grid_values.shape, jnp.bfloat16),
        scratch_shapes=[pltpu.VMEM((slots * (4 * block + 1), wide), jnp.float32)],
        compiler_params=params(1),
        cost_estimate=cost(
            rows * lats * lons * slots * 4, rows * lats * lons * 4 + slots * rows * wide * 8
        ),
    )(*operands, table, grid_values)


PIECES = (3, 2)


def pieces_of(count):
    cuts, at = [], 0
    for size in PIECES:
        if at < count:
            cuts.append((at, min(count, at + size)))
            at += size
    if at < count:
        cuts.append((at, count))
    return cuts


def pick(table, rows):
    hit = rows[:, None] == jnp.arange(table.shape[0], dtype=jnp.int32)[None, :]
    hit = hit.reshape(hit.shape + (1,) * (table.ndim - 1))
    return jnp.sum(jnp.where(hit, table[None], 0), axis=1)


def local(
    grid_values,
    legendre,
    gauss_weights,
    modes_in,
    modes_out,
    stiffness,
    slot_pair,
    lat_order,
    field_slots,
):
    rows, lats, lons = grid_values.shape
    slots = legendre.shape[0]
    wave_size, lev_size = lax.axis_size("wave"), lax.axis_size("lev")
    wave_rank, lev_rank = lax.axis_index("wave"), lax.axis_index("lev")
    waves = 2 * slot_pair.shape[0]
    parts = math.gcd(slots, 8)
    chunks = slots // parts
    keep = round_up(waves + 1, 16)
    wide = round_up(lats, 128) if lats > 64 else round_up(lats, 32)
    depth = 4 * rows
    pieces = pieces_of(chunks)

    slot_at, owner_at = [], []
    for low, high in pieces:
        for u in range(wave_size):
            slot_at += range(low * parts, high * parts)
            owner_at += [u] * ((high - low) * parts)
    owner = wave_rank ^ jnp.array(owner_at, dtype=jnp.int32)
    pairs = pick(slot_pair, owner * slots + jnp.array(slot_at, dtype=jnp.int32))
    mirrored = waves - 1 - pairs
    odd_pair = (pairs & 1) == 1
    table = half_table(
        jnp.stack([jnp.where(odd_pair, mirrored, pairs), jnp.where(odd_pair, pairs, mirrored)]), lons
    )

    lat_blocks = jnp.pad(
        lat_order.reshape(wave_size, lats), ((0, 0), (0, wide - lats)), constant_values=-1
    )
    relative = wave_rank ^ jnp.arange(wave_size, dtype=jnp.int32)
    chosen = pick(lat_blocks, relative).reshape(1, -1)
    own_lats = pick(lat_blocks, wave_rank.reshape(1)).reshape(-1)
    row_weight = jnp.sum(
        jnp.where(
            own_lats[None, :] == jnp.arange(lat_order.shape[0], dtype=jnp.int32)[:, None],
            gauss_weights[:, None],
            0.0,
        ),
        axis=0,
        keepdims=True,
    )
    counts = [(high - low) * parts for low, high in pieces for _ in range(wave_size)]
    made = list(fourier(grid_values, table, row_weight, counts, wide))
    routes = [[(i, i ^ u) for i in range(wave_size)] for u in range(wave_size)]

    def exchange(blocks):
        return [blocks[0]] + [lax.ppermute(blocks[u], "wave", routes[u]) for u in range(1, wave_size)]

    coefficients = []
    for piece, (low, high) in enumerate(pieces):
        blocks = made[piece * wave_size : (piece + 1) * wave_size]
        shape = (high - low, parts, depth, wide)
        coefficients.append(exchange([block.reshape(shape) for block in blocks]))

    basis = ordered_basis(
        legendre, chosen, keep, chunks, jnp.zeros((1,), jnp.int32), parts, [made[0]]
    )
    basis = basis.reshape(chunks, parts, keep, -1)
    into, out_of, stiff = matrices(field_slots, modes_in, modes_out, stiffness, lev_size)
    rank = lev_rank.reshape(1)

    count = len(pieces)
    earlier = []
    arrived, returned, back = [None] * count, [None] * count, [None] * count

    def to_modes(piece):
        low, high = pieces[piece]
        flat = (high - low) * (parts // 2) * keep
        padded = round_up(flat, lev_size * 8)
        base = low * wave_size * parts
        spectral = sums(waves, base, pairs, coefficients[piece], basis, low, earlier)
        earlier[:] = [spectral]
        spectral = spectral.reshape(flat, depth)
        if padded > flat:
            spectral = jnp.pad(spectral, ((0, padded - flat), (0, 0)))
        arrived[piece] = lax.all_to_all(
            spectral.reshape(lev_size, -1, depth), "lev", split_axis=0, concat_axis=0, tiled=True
        )

    def solved(piece):
        low, high = pieces[piece]
        base = low * wave_size * parts
        held = (high - low) * (parts // 2)
        made = solve(
            waves, base, keep, held, rank, pairs, arrived[piece], into, out_of, stiff, earlier
        )
        earlier[:] = [made]
        returned[piece] = lax.all_to_all(made, "lev", split_axis=0, concat_axis=0, tiled=True)

    def to_waves(piece):
        low, high = pieces[piece]
        steps = high - low
        base = low * wave_size * parts
        implicit = returned[piece].reshape(-1, depth)[: steps * (parts // 2) * keep]
        implicit = implicit.reshape(steps, parts // 2, keep, depth)
        made = fields(waves, base, pairs, implicit, basis, low, wave_size, earlier)
        earlier[:] = [made[0]]
        back[piece] = exchange(made)

    to_modes(0)
    for piece in range(count):
        solved(piece)
        if piece + 1 < count:
            to_modes(piece + 1)
        if piece:
            earlier += back[piece - 1][1:-1]
        to_waves(piece)
    operands = [block for blocks in back for block in blocks]
    return grid_product(operands, table, grid_values, wide)


def solution(mesh):
    in_specs = (P("lev", "wave", None), P("wave", None, None), P(), P(), P(), P(), P(), P(), P())
    out_specs = P("lev", "wave", None)
    return jax.shard_map(local, mesh=mesh, in_specs=in_specs, out_specs=out_specs, check_vma=False)
```
